256 devices in a mesh: blk: 8 (over y, x_lo), group: 32 (over x_hi, z, core).
Axes of the slice: x: 4 (x_hi: 2, x_lo: 2; x = x_hi * 2 + x_lo), y: 4, z: 8, core: 2. Of those that a mesh axis runs over, the one named last changes fastest.
Arguments:
- patches: bfloat16 [65536, 1152], P(('blk', 'group')), may hold values from -400 to 400
- row_owner: int32 [8, 32, 256], P('blk'), may hold values from 0 to 31, as said below
- row_slot: int32 [8, 32, 256], P('blk'), may hold values from 0 to 3, as said below
- text_embed: bfloat16 [1024, 1152], P(('blk', 'group')), may hold values from -6 to 6
- probe_query: float32 [1152], replicated, may hold values from -5 to 5
- w_key: bfloat16 [1152, 1152], replicated, may hold values from -0.1875 to 0.1875
- w_value: bfloat16 [1152, 1152], replicated, may hold values from -0.1875 to 0.1875
- w_out: bfloat16 [1152, 1152], replicated, may hold values from -0.1875 to 0.1875
- logit_scale: float32 [1], replicated, may hold values from 1.6 to 2.3
- logit_bias: float32 [1], replicated, may hold values from -1.5 to -0.5
Outputs:
- grad_patches: bfloat16 [65536, 1152], P(('blk', 'group'))
- grad_text: bfloat16 [1024, 1152], P(('blk', 'group'))
The draws below stay inside these ranges and needn't reach their ends.
Inputs may be any that keep to these rules, and one draw needn't show every extreme that they name: `row_owner`: in each blk index, the rows of one device name one owner at most 24 times; in every draw some owner of each blk index is named exactly 24 times by every device of that blk index. `row_slot`: every slot of every owner receives at least one row of its blk index.
All inputs are finite; a program needn't handle non-finite values.
Results may differ from the reference program's by a relative error of at most 0.002.
Values may be sent and summed in bfloat16 or wider, within the bound.
A program may use at most 128 MiB of HBM per device.

```python
import math
import jax
import jax.numpy as jnp
from jax import lax

D = 1152
HEADS = 16
HEAD_DIM = 72
IMG_DEV = 4
PSRC = 256
CAP = 24
IMAGES = 1024
ROWS = 65536
N_BLK = 8
N_GROUP = 32


def layout(key):
    hot_key, shift_key, spread_key, order_key = jax.random.split(key, 4)
    hot = jax.random.randint(hot_key, (N_BLK, 1, 1), 0, N_GROUP)
    spots = jnp.arange(PSRC, dtype=jnp.int32)[None, None, :]
    beyond = jnp.maximum(spots - CAP, 0)
    owner = jnp.where(spots < CAP, hot, (hot + 1 + beyond % (N_GROUP - 1)) % N_GROUP)
    rank = jnp.where(spots < CAP, spots, beyond // (N_GROUP - 1))
    offset = jax.random.randint(shift_key, (N_BLK, N_GROUP, 1), 0, IMG_DEV)
    spread = jax.random.randint(spread_key, (N_BLK, N_GROUP, PSRC), 0, IMG_DEV)
    slot = jnp.where(rank < IMG_DEV, (rank + offset) % IMG_DEV, spread)
    owner = jnp.broadcast_to(owner, (N_BLK, N_GROUP, PSRC))
    ranking = jax.random.randint(order_key, (N_BLK, N_GROUP, PSRC), 0, 2 ** 19) * 2048 + spots
    order = jnp.argsort(ranking, axis=2)
    return (jnp.take_along_axis(owner, order, axis=2).astype(jnp.int32), jnp.take_along_axis(slot, order, axis=2).astype(jnp.int32))


def draw_row_owner(key, part):
    return layout(key)[0]


def draw_row_slot(key, part):
    return layout(key)[1]


def draw_patches(key, part):
    key = jax.random.fold_in(key, 7)
    base_key = jax.random.fold_in(key, 0)
    base = jax.random.normal(base_key, (ROWS, D), jnp.float32)
    values = base
    return jnp.clip(values, -400.0, 400.0).astype(jnp.bfloat16)


def level_of(own_key, dims, pieces, smallest, largest):
    loudness = 1.0
    for dim, shards_of in pieces:
        steps = jax.random.uniform(jax.random.fold_in(jax.random.fold_in(own_key, 6), dim), (shards_of,), jnp.float32, smallest / len(pieces), largest / len(pieces))
        loudness = loudness * jnp.repeat(jnp.exp(steps), dims[dim] // shards_of).reshape((-1,) + (1,) * (len(dims) - 1 - dim))
    return loudness


def centred(key, extent, deviation, reach, cuts=(), kind=jnp.bfloat16):
    factor_of = level_of(key, extent, cuts, -0.22, 0.18) if cuts else 1.0
    entries = jax.random.normal(key, extent, jnp.float32) * deviation * factor_of
    return jnp.minimum(jnp.maximum(entries, -reach), reach).astype(kind)


def setup_inputs(seed: int = 0) -> dict:
    streams_of = jax.random.split(jax.random.key(seed), 11)
    patches = draw_patches(jax.random.fold_in(streams_of[10], 71), 0)
    row_owner = draw_row_owner(jax.random.fold_in(streams_of[10], 71), 0)
    row_slot = draw_row_slot(jax.random.fold_in(streams_of[10], 71), 0)
    text_embed = centred(streams_of[3], (IMAGES, D), 1.0, 6.0, ((0, 256),))
    probe_query = centred(streams_of[4], (D,), 1.0, 5.0, (), jnp.float32)
    w_key = centred(streams_of[5], (D, D), D ** -0.5, 0.1875)
    w_value = centred(streams_of[6], (D, D), D ** -0.5, 0.1875)
    w_out = centred(streams_of[7], (D, D), D ** -0.5, 0.1875)
    logit_scale = jnp.clip(jax.random.uniform(streams_of[8], (1,), jnp.float32, 1.6, 2.3), 1.6, 2.3)
    logit_bias = jnp.clip(jax.random.uniform(streams_of[9], (1,), jnp.float32, -1.5, -0.5), -1.5, -0.5)
    return {"patches": patches, "row_owner": row_owner, "row_slot": row_slot, "text_embed": text_embed, "probe_query": probe_query, "w_key": w_key, "w_value": w_value, "w_out": w_out, "logit_scale": logit_scale, "logit_bias": logit_bias}


loss_scale = 256.0
norm_eps = 1e-06
highest = lax.Precision.HIGHEST

def unit_rows(matrix):
    length = jnp.sqrt(lax.optimization_barrier(jnp.sum(matrix * matrix, axis=-1, keepdims=True)) + norm_eps)
    return (matrix / length, length)

def reference(patches, row_owner, row_slot, text_embed, probe_query, w_key, w_value, w_out, logit_scale, logit_bias):
    span = N_GROUP * IMG_DEV
    block_rows = N_GROUP * PSRC
    query_scaled = probe_query / math.sqrt(HEAD_DIM)
    query_heads = query_scaled.reshape(HEADS, HEAD_DIM)
    query_table = (jnp.eye(HEADS, dtype=jnp.float32)[:, :, None] * query_heads[None, :, :]).reshape(HEADS, D)
    key_probe = jnp.dot(w_key.astype(jnp.float32), query_table.T, precision=highest)
    value_table = w_value.astype(jnp.float32).reshape(D, HEADS, HEAD_DIM)
    rows_by_block = patches.reshape(N_BLK, block_rows, D)
    ids_by_block = (row_owner * IMG_DEV + row_slot).reshape(N_BLK, block_rows).astype(jnp.int32)

    def pool_weights(rows, ids):
        scores = jnp.dot(rows, key_probe, precision=highest)
        peak = jax.ops.segment_max(scores, ids, num_segments=span)
        raised = jnp.exp(scores - peak[ids])
        totals = jax.ops.segment_sum(raised, ids, num_segments=span)
        return raised / totals[ids]

    def forward(pair):
        rows = pair[0].astype(jnp.float32)
        ids = pair[1]
        weights = pool_weights(rows, ids)

        def head_mix(head):
            column = lax.dynamic_index_in_dim(weights, head, 1, keepdims=True)
            return jax.ops.segment_sum(column * rows, ids, num_segments=span)
        mixed = lax.map(head_mix, jnp.arange(HEADS, dtype=jnp.int32))
        pooled = jnp.einsum('hne,ehd->nhd', mixed, value_table, precision=highest)
        return pooled.reshape(span, D)
    pooled = lax.map(forward, (rows_by_block, ids_by_block)).reshape(IMAGES, D)
    embeds = jnp.dot(pooled, w_out.astype(jnp.float32), precision=highest)
    image_unit, image_norm = unit_rows(embeds)
    text_unit, text_norm = unit_rows(text_embed.astype(jnp.float32))
    temper = jnp.exp(logit_scale[0])

    def logit_block(carry, pair):
        units, first = pair
        logits = temper * jnp.dot(units, text_unit.T, precision=highest) + logit_bias[0]
        positive = (jnp.arange(IMAGES, dtype=jnp.int32)[None, :] == first + jnp.arange(span, dtype=jnp.int32)[:, None]).astype(jnp.float32)
        grads = loss_scale * (jax.nn.sigmoid(logits) - positive)
        image_part = temper * jnp.dot(grads, text_unit, precision=highest)
        return (carry + temper * jnp.dot(grads.T, units, precision=highest), image_part)
    firsts = (jnp.arange(N_BLK, dtype=jnp.int32) * span).astype(jnp.int32)
    text_dunit, image_dunit = lax.scan(logit_block, jnp.zeros((IMAGES, D), jnp.float32), (image_unit.reshape(N_BLK, span, D), firsts))
    image_dunit = image_dunit.reshape(IMAGES, D)
    grad_text = ((text_dunit - text_unit * lax.optimization_barrier(jnp.sum(text_unit * text_dunit, axis=1, keepdims=True))) / text_norm).astype(jnp.bfloat16)
    embed_grad = (image_dunit - image_unit * lax.optimization_barrier(jnp.sum(image_unit * image_dunit, axis=1, keepdims=True))) / image_norm
    pooled_grad = jnp.dot(embed_grad, w_out.astype(jnp.float32).T, precision=highest).reshape(N_BLK, span, HEADS, HEAD_DIM)

    def backward(triple):
        rows = triple[0].astype(jnp.float32)
        ids = triple[1]
        grad_heads = triple[2]
        weights = pool_weights(rows, ids)
        value_probe = jnp.einsum('ehd,nhd->hne', value_table, grad_heads, precision=highest)

        def head_terms(carry, head):
            picked = lax.dynamic_index_in_dim(value_probe, head, 0, keepdims=False)[ids]
            column = lax.dynamic_index_in_dim(weights, head, 1, keepdims=True)
            return (carry + column * picked, lax.optimization_barrier(jnp.sum(rows * picked, axis=1)))
        value_part, dweights = lax.scan(head_terms, jnp.zeros((block_rows, D), jnp.float32), jnp.arange(HEADS, dtype=jnp.int32))
        dweights = dweights.T
        mass = jax.ops.segment_sum(weights * dweights, ids, num_segments=span)
        dscores = weights * (dweights - mass[ids])
        key_part = jnp.dot(dscores, key_probe.T, precision=highest)
        return (key_part + value_part).astype(jnp.bfloat16)
    grad_patches = lax.map(backward, (rows_by_block, ids_by_block, pooled_grad)).reshape(ROWS, D)
    return (grad_patches, grad_text)
```

```python
import functools
import math

import jax
import jax.numpy as jnp
from jax import lax
from jax.experimental import pallas as pl
from jax.experimental.pallas import tpu as pltpu
from jax.sharding import PartitionSpec as P

HEADS = 16
IMG = 4
LANES = 128
CHUNK = 384
LOSS_SCALE = 256.0
EPS = 1e-06
LOW = -1e30

F32 = jnp.float32
BF16 = jnp.bfloat16
MESH = pl.DeviceIdType.MESH


def mm(a, b):
    return lax.dot_general(a, b, (((1,), (0,)), ((), ())), preferred_element_type=F32)


def mm_nt(a, b):
    return lax.dot_general(a, b, (((1,), (1,)), ((), ())), preferred_element_type=F32)


def pieces(x, count):
    out = []
    for _ in range(count - 1):
        top = x.astype(BF16).astype(F32)
        out.append(top)
        x = x - top
    out.append(x.astype(BF16).astype(F32))
    return out


def stacked(x, count):
    return jnp.concatenate(pieces(x, count), axis=0).astype(BF16)


def small_rows(x, buf):
    for k, piece in enumerate(pieces(x, 3)):
        buf[k * IMG : (k + 1) * IMG, :] = piece
    return buf[...].astype(BF16)


def three(y):
    return y[0:IMG] + y[IMG : 2 * IMG] + y[2 * IMG : 3 * IMG]


def kernel(
    nb,
    ng,
    nz,
    patches,
    owner,
    slot,
    text,
    probe,
    w_key,
    w_value,
    w_out,
    logit_scale,
    logit_bias,
    g_patch,
    g_text,
    wk,
    wv,
    wo,
    p,
    v,
    st,
    hm,
    kp3,
    kpr,
    ot,
    et,
    acc_out,
    acc_in,
    fs,
    rows16,
    pooled_buf,
    unit_all,
    u32,
    di_out,
    di_in,
    t_all,
    tf,
    t_out,
    t_in,
    pg_all,
    pgm,
    ob,
    vg,
    load_sem,
    pair_send,
    pair_recv,
    text_send,
    text_recv,
    acc_send,
    acc_recv,
    unit_send,
    unit_recv,
    di_send,
    di_recv,
    td_send,
    td_recv,
    pg_send,
    pg_recv,
):
    nq = ng // 2
    nxh = nq // nz
    nplane = nb * nxh * 2
    mine = nq * IMG
    rows, width = patches.shape
    chunks = width // CHUNK
    head_width = width // HEADS
    blk = lax.axis_index("blk")
    grp = lax.axis_index("group")
    core = grp % 2
    q = grp // 2
    z = q % nz
    xh = q // nz
    sib = q * 2 + (1 - core)
    place = (blk * nxh + xh) * 2 + core

    def group_peer(d):
        k = (q + d) % nq
        return k, (blk, k * 2 + core)

    def line_peer(d):
        k = (z + d) % nz
        return k, (blk, (xh * nz + k) * 2 + core)

    def plane_peer(d):
        k = (place + d) % nplane
        return k, (k // (2 * nxh), (((k // 2) % nxh) * nz + z) * 2 + k % 2)

    def remote(src, dst, send, recv, device):
        return pltpu.make_async_remote_copy(
            src_ref=src,
            dst_ref=dst,
            send_sem=send,
            recv_sem=recv,
            device_id=device,
            device_id_type=MESH,
        )

    def each(count, act):
        def step(d, carry):
            act(d)
            return carry

        lax.fori_loop(1, count, step, 0)

    def spread(peer, count, src_of, dst, me, send, recv):
        def act(d):
            k, device = peer(d)
            remote(src_of(k), dst.at[me], send.at[k], recv.at[me], device).start()

        each(count, act)

    def gather_wait(peer, count, dst, send, recv):
        def act(d):
            k, device = peer(d)
            remote(dst.at[k], dst.at[k], send.at[k], recv.at[k], device).wait_recv()

        each(count, act)

    def send_wait(peer, count, src_of, send, recv):
        def act(d):
            k, device = peer(d)
            remote(src_of(k), src_of(k), send.at[k], recv.at[k], device).wait_send()

        each(count, act)

    load_k = pltpu.make_async_copy(w_key, wk, load_sem.at[0])
    load_p = pltpu.make_async_copy(patches, p.at[0], load_sem.at[1])
    load_v = pltpu.make_async_copy(w_value, wv, load_sem.at[2])
    load_o = pltpu.make_async_copy(w_out, wo, load_sem.at[3])
    load_k.start()
    load_p.start()
    load_v.start()
    load_o.start()

    barrier = pltpu.get_barrier_semaphore()

    def greet(peer):
        def act(d):
            pl.semaphore_signal(barrier, inc=1, device_id=peer(d)[1], device_id_type=MESH)

        return act

    each(nplane, greet(plane_peer))
    each(nq, greet(group_peer))

    row_i = lax.broadcasted_iota(jnp.int32, (LANES, width), 0)
    col_i = lax.broadcasted_iota(jnp.int32, (LANES, width), 1)
    first = (row_i & (HEADS - 1)) * head_width
    in_head = (col_i >= first) & (col_i < first + head_width)
    hm[...] = jnp.where(in_head & (row_i < 3 * HEADS), 1.0, 0.0).astype(BF16)
    q3 = pieces(probe[...] / math.sqrt(head_width), 3)
    band = lax.broadcasted_iota(jnp.int32, (3 * HEADS, width), 0) // HEADS
    q_rows = jnp.where(band == 0, q3[0], jnp.where(band == 1, q3[1], q3[2]))
    table = (q_rows * hm[0 : 3 * HEADS, :].astype(F32)).astype(BF16)
    load_k.wait()
    kpt = mm_nt(table, wk[...])
    kp = kpt[0:HEADS] + kpt[HEADS : 2 * HEADS] + kpt[2 * HEADS : 3 * HEADS]
    kp_pieces = pieces(kp, 3)
    kp3[...] = jnp.concatenate(kp_pieces, axis=0).astype(BF16)
    kpr[...] = jnp.zeros_like(kpr)
    kpr[3 * HEADS : 6 * HEADS, :] = jnp.concatenate(
        [kp_pieces[0], kp_pieces[1], kp_pieces[0]], axis=0
    ).astype(BF16)

    pl.semaphore_wait(barrier, nplane - 1 + nq - 1)
    pair = remote(patches, p.at[1], pair_send.at[0], pair_recv.at[0], (blk, sib))
    pair.start()
    t_all[place] = text[...]
    spread(plane_peer, nplane, lambda k: text, t_all, place, text_send, text_recv)

    def project(part):
        s = mm_nt(kp3[...], p[part])
        st[:, part * rows : (part + 1) * rows] = (
            s[0:HEADS] + s[HEADS : 2 * HEADS] + s[2 * HEADS : 3 * HEADS]
        )

        def step(j, carry):
            cols = pl.ds(pl.multiple_of(j * CHUNK, CHUNK), CHUNK)
            v[part, :, cols] = mm(p[part], wv[:, cols])
            return carry

        lax.fori_loop(0, chunks, step, 0)

    load_p.wait()
    load_v.wait()
    project(0)
    own_owner = owner[0, pl.ds(grp, 1), :]
    own_slot = slot[0, pl.ds(grp, 1), :]
    own_id = own_owner * IMG + own_slot
    sib_id = owner[0, pl.ds(sib, 1), :] * IMG + slot[0, pl.ds(sib, 1), :]
    pair.wait_recv()
    project(1)

    ids = jnp.concatenate([own_id, sib_id], axis=1)
    img_i = lax.broadcasted_iota(jnp.int32, (mine, 2 * rows), 0)
    member = ids == (img_i >> 2) * (2 * IMG) + core * IMG + (img_i & (IMG - 1))
    ot[...] = jnp.where(member, 1.0, 0.0).astype(BF16)
    valid = ((ids >> 2) & 1) == core
    scores = st[...]
    lane = lax.broadcasted_iota(jnp.int32, (mine, LANES), 1)
    peak = jnp.zeros((mine, LANES), F32)
    for h in range(HEADS):
        top = jnp.max(jnp.where(member, scores[h : h + 1, :], LOW), axis=1, keepdims=True)
        peak = jnp.where(lane == h, top, peak)
    peak_t = jnp.transpose(peak)[0:HEADS]
    shift = mm(stacked(peak_t, 3), ot[...])
    shift = shift[0:HEADS] + shift[HEADS : 2 * HEADS] + shift[2 * HEADS : 3 * HEADS]
    e = jnp.where(valid, jnp.exp(scores - shift), 0.0)
    e_hi, e_lo = pieces(e, 2)
    e_pad = jnp.concatenate(
        [
            jnp.zeros((HEADS, 2 * rows), F32),
            e_hi,
            e_lo,
            jnp.zeros((LANES - 3 * HEADS, 2 * rows), F32),
        ],
        axis=0,
    )
    et[...] = jnp.transpose(e_pad).astype(BF16)
    stats = jnp.where(lane < HEADS, peak, mm(ot[...], et[...]))
    for k in range(nq):
        acc_out[k, :, width : width + LANES] = stats[k * IMG : (k + 1) * IMG]

    def pool(j, carry):
        cols = pl.ds(pl.multiple_of(j * CHUNK, CHUNK), CHUNK)
        spread_e = mm(et[...], hm[:, cols])
        total = jnp.zeros((mine, CHUNK), F32)
        for part in range(2):
            here = slice(part * rows, (part + 1) * rows)
            x_hi, x_lo = pieces(spread_e[here] * v[part, :, cols], 2)
            total += mm(ot[:, here], x_hi.astype(BF16)) + mm(ot[:, here], x_lo.astype(BF16))
        for k in range(nq):
            acc_out[k, :, cols] = total[k * IMG : (k + 1) * IMG]
        return carry

    lax.fori_loop(0, chunks, pool, 0)
    spread(group_peer, nq, lambda k: acc_out.at[k], acc_in, q, acc_send, acc_recv)
    acc_in[q] = acc_out[q]

    gather_wait(plane_peer, nplane, t_all, text_send, text_recv)
    for k in range(nplane):
        tf[k * IMG : (k + 1) * IMG, :] = t_all[k].astype(F32)
    texts = tf[...]
    tb = texts.astype(BF16)
    inv = 1.0 / jnp.sqrt(jnp.sum(texts * texts, axis=1, keepdims=True) + EPS)
    inv_row = jnp.transpose(jnp.broadcast_to(inv, (nplane * IMG, LANES)))[0:1, :]
    own_code = (own_owner & 1) * mine + (own_owner >> 1) * IMG + own_slot
    code_i = lax.broadcasted_iota(jnp.int32, (2 * mine, rows), 0)
    own_ot = jnp.where(own_code == code_i, 1.0, 0.0)
    own_o = jnp.transpose(own_ot).astype(BF16)
    ob[:, 0 : 2 * mine] = own_o
    ob[:, 2 * mine : 4 * mine] = own_o
    rows16[...] = jnp.zeros_like(rows16)
    load_o.wait()

    gather_wait(group_peer, nq, acc_in, acc_send, acc_recv)
    lane4 = lax.broadcasted_iota(jnp.int32, (IMG, LANES), 1)
    heads4 = lane4 < HEADS
    parts = [acc_in[k, :, width : width + LANES] for k in range(nq)]
    m = parts[0]
    for part in parts[1:]:
        m = jnp.maximum(m, part)
    factors = []
    denom = jnp.zeros((IMG, LANES), F32)
    for part in parts:
        f = jnp.exp(part - m)
        mass = pltpu.roll(part, LANES - HEADS, 1) + pltpu.roll(part, LANES - 2 * HEADS, 1)
        factors.append(f)
        denom = denom + f * mass
    denom = jnp.where(heads4, denom, 1.0)
    lse = m + jnp.log(denom)
    for k, f in enumerate(factors):
        f_hi, f_lo = pieces(jnp.where(heads4, f / denom, 0.0), 2)
        fs[k * IMG : (k + 1) * IMG, :] = f_hi + pltpu.roll(f_lo, HEADS, 1)
    factor = mm(fs[...].astype(BF16), hm[...])
    pooled = jnp.zeros((IMG, width), F32)
    for k in range(nq):
        pooled = pooled + factor[k * IMG : (k + 1) * IMG] * acc_in[k, :, 0:width]
    pooled_buf[...] = pooled
    embeds = three(mm(small_rows(pooled, rows16), wo[...]))
    norm = jnp.sqrt(jnp.sum(embeds * embeds, axis=1, keepdims=True) + EPS)
    unit = embeds / norm
    unit_all[z] = unit
    spread(line_peer, nz, lambda k: unit_all.at[z], unit_all, z, unit_send, unit_recv)

    gather_wait(line_peer, nz, unit_all, unit_send, unit_recv)
    for k in range(nz):
        u32[k * IMG : (k + 1) * IMG, :] = unit_all[k]
    nimg = nz * IMG
    ntext = nplane * IMG
    u_pieces = pieces(u32[...], 3)
    dots = mm_nt(jnp.concatenate(u_pieces, axis=0).astype(BF16), tb)
    dots = dots[0:nimg] + dots[nimg : 2 * nimg] + dots[2 * nimg : 3 * nimg]
    temper = jnp.exp(jnp.full((1, 1), logit_scale[0], F32))
    logits = temper * (dots * inv_row) + logit_bias[0]
    block_row = lax.broadcasted_iota(jnp.int32, (nimg, ntext), 0)
    block_col = lax.broadcasted_iota(jnp.int32, (nimg, ntext), 1)
    positive = ((block_row >> 2) == z) & (block_col - place * IMG == (block_row & (IMG - 1)))
    signal = 1.0 / (1.0 + jnp.exp(-logits)) - jnp.where(positive, 1.0, 0.0)
    di = mm(stacked(signal * inv_row, 3), tb)
    di = di[0:nimg] + di[nimg : 2 * nimg] + di[2 * nimg : 3 * nimg]
    for k in range(nz):
        di_out[k] = di[k * IMG : (k + 1) * IMG]
    spread(line_peer, nz, lambda k: di_out.at[k], di_in, z, di_send, di_recv)
    di_in[z] = di_out[z]

    s_hi, s_lo = pieces(signal, 2)
    s_pad = jnp.concatenate(
        [s_hi, s_hi, s_lo, jnp.zeros((LANES - 3 * nimg, ntext), F32)], axis=0
    )
    s_t = jnp.transpose(s_pad).astype(BF16)
    u_pad = jnp.concatenate(
        [u_pieces[0], u_pieces[1], u_pieces[0], jnp.zeros((LANES - 3 * nimg, width), F32)], axis=0
    ).astype(BF16)
    td = mm(s_t, u_pad)
    for k in range(nplane):
        t_out[k] = td[k * IMG : (k + 1) * IMG]
    spread(plane_peer, nplane, lambda k: t_out.at[k], t_in, place, td_send, td_recv)
    t_in[place] = t_out[place]

    gather_wait(line_peer, nz, di_in, di_send, di_recv)
    dunit = di_in[0]
    for k in range(1, nz):
        dunit = dunit + di_in[k]
    dunit = dunit * (temper * LOSS_SCALE)
    unit = unit_all[z]
    embed_grad = (dunit - unit * jnp.sum(unit * dunit, axis=1, keepdims=True)) / norm
    pooled_grad = three(mm_nt(small_rows(embed_grad, rows16), wo[...]))
    mass = three(mm_nt(small_rows(pooled_grad * pooled_buf[...], rows16), hm[...]))
    pg_all[core, q, :, 0:width] = pooled_grad
    pg_all[core, q, :, width : width + LANES] = jnp.where(
        heads4, lse, jnp.where(lane4 < 2 * HEADS, mass, 0.0)
    )
    own_half = pg_all.at[core]
    spread(group_peer, nq, lambda k: own_half.at[q], own_half, q, pg_send, pg_recv)

    gather_wait(plane_peer, nplane, t_in, td_send, td_recv)
    text_dunit = t_in[0]
    for k in range(1, nplane):
        text_dunit = text_dunit + t_in[k]
    text_dunit = text_dunit * (temper * LOSS_SCALE)
    own_text = text[...].astype(F32)
    text_norm = jnp.sqrt(jnp.sum(own_text * own_text, axis=1, keepdims=True) + EPS)
    text_unit = own_text / text_norm
    g_text[...] = (
        (text_dunit - text_unit * jnp.sum(text_unit * text_dunit, axis=1, keepdims=True))
        / text_norm
    ).astype(BF16)

    gather_wait(group_peer, nq, own_half, pg_send, pg_recv)
    swap = remote(pg_all.at[core], pg_all.at[core], pair_send.at[1], pair_recv.at[1], (blk, sib))
    swap.start()
    swapped = remote(
        pg_all.at[1 - core], pg_all.at[1 - core], pair_send.at[1], pair_recv.at[1], (blk, sib)
    )
    swapped.wait_recv()

    for c in range(2):
        for k in range(nq):
            at = (c * nq + k) * IMG
            pgm[at : at + IMG, :] = pg_all[c, k]
    row_stats = stacked(jnp.transpose(pgm[:, width : width + LANES])[0 : 2 * HEADS], 3)
    row_stats = mm(row_stats, own_ot.astype(BF16))
    row_stats = (
        row_stats[0 : 2 * HEADS] + row_stats[2 * HEADS : 4 * HEADS] + row_stats[4 * HEADS : 6 * HEADS]
    )
    pgr = mm(ob[...], stacked(pgm[:, 0:width], 2))
    d_hi, d_lo = pieces(pgr * v[0], 2)
    dw = mm_nt(hm[0:HEADS, :], d_hi.astype(BF16)) + mm_nt(hm[0:HEADS, :], d_lo.astype(BF16))
    w = jnp.exp(st[:, 0:rows] - row_stats[0:HEADS])
    ds = w * (dw - row_stats[HEADS : 2 * HEADS])
    w_hi, w_lo = pieces(w, 2)
    ds_hi, ds_lo = pieces(ds, 2)
    blank = jnp.zeros((HEADS, rows), F32)
    wt = jnp.transpose(
        jnp.concatenate([w_hi, w_lo, blank, ds_hi, ds_hi, ds_lo, blank, blank], axis=0)
    ).astype(BF16)
    vg[...] = stacked(mm(wt, hm[...]) * pgr, 2)
    et[0:rows, :] = wt

    def back(j, carry):
        cols = pl.ds(pl.multiple_of(j * CHUNK, CHUNK), CHUNK)
        g = mm_nt(vg[...], wv[cols, :])
        g_patch[:, cols] = (g[0:rows] + g[rows : 2 * rows] + mm(et[0:rows, :], kpr[:, cols])).astype(
            BF16
        )
        return carry

    lax.fori_loop(0, chunks, back, 0)

    pair.wait_send()
    swap.wait_send()
    send_wait(plane_peer, nplane, lambda k: text, text_send, text_recv)
    send_wait(group_peer, nq, lambda k: acc_out.at[k], acc_send, acc_recv)
    send_wait(line_peer, nz, lambda k: unit_all.at[z], unit_send, unit_recv)
    send_wait(line_peer, nz, lambda k: di_out.at[k], di_send, di_recv)
    send_wait(plane_peer, nplane, lambda k: t_out.at[k], td_send, td_recv)
    send_wait(group_peer, nq, lambda k: own_half.at[q], pg_send, pg_recv)


def local(nb, ng, nz, patches, owner, slot, text, probe, w_key, w_value, w_out, scale, bias):
    rows, width = patches.shape
    nq = ng // 2
    nplane = nb * (nq // nz) * 2
    mine = nq * IMG
    vmem = pl.BlockSpec(memory_space=pltpu.VMEM)
    smem = pl.BlockSpec(memory_space=pltpu.SMEM)
    anywhere = pl.BlockSpec(memory_space=pl.ANY)
    weight = pltpu.VMEM((width, width), BF16)
    dma = pltpu.SemaphoreType.DMA
    return pl.pallas_call(
        functools.partial(kernel, nb, ng, nz),
        out_shape=(
            jax.ShapeDtypeStruct((rows, width), BF16),
            jax.ShapeDtypeStruct((IMG, width), BF16),
        ),
        in_specs=[anywhere, vmem, vmem, vmem, vmem, anywhere, anywhere, anywhere, smem, smem],
        out_specs=(vmem, vmem),
        scratch_shapes=[
            weight,
            weight,
            weight,
            pltpu.VMEM((2, rows, width), BF16),
            pltpu.VMEM((2, rows, width), F32),
            pltpu.VMEM((HEADS, 2 * rows), F32),
            pltpu.VMEM((LANES, width), BF16),
            pltpu.VMEM((3 * HEADS, width), BF16),
            pltpu.VMEM((LANES, width), BF16),
            pltpu.VMEM((mine, 2 * rows), BF16),
            pltpu.VMEM((2 * rows, LANES), BF16),
            pltpu.VMEM((nq, IMG, width + LANES), F32),
            pltpu.VMEM((nq, IMG, width + LANES), F32),
            pltpu.VMEM((mine, LANES), F32),
            pltpu.VMEM((16, width), F32),
            pltpu.VMEM((IMG, width), F32),
            pltpu.VMEM((nz, IMG, width), F32),
            pltpu.VMEM((nz * IMG, width), F32),
            pltpu.VMEM((nz, IMG, width), F32),
            pltpu.VMEM((nz, IMG, width), F32),
            pltpu.VMEM((nplane, IMG, width), BF16),
            pltpu.VMEM((nplane * IMG, width), F32),
            pltpu.VMEM((nplane, IMG, width), F32),
            pltpu.VMEM((nplane, IMG, width), F32),
            pltpu.VMEM((2, nq, IMG, width + LANES), F32),
            pltpu.VMEM((2 * mine, width + LANES), F32),
            pltpu.VMEM((rows, 4 * mine), BF16),
            pltpu.VMEM((2 * rows, width), BF16),
            dma((4,)),
            dma((2,)),
            dma((2,)),
            dma((nplane,)),
            dma((nplane,)),
            dma((nq,)),
            dma((nq,)),
            dma((nz,)),
            dma((nz,)),
            dma((nz,)),
            dma((nz,)),
            dma((nplane,)),
            dma((nplane,)),
            dma((nq,)),
            dma((nq,)),
        ],
        compiler_params=pltpu.CompilerParams(
            collective_id=0, has_side_effects=True, vmem_limit_bytes=56 * 2**20
        ),
        name="pool_contrast",
    )(patches, owner, slot, text, probe.reshape(1, width), w_key, w_value, w_out, scale, bias)


def solution(mesh):
    nb = mesh.shape["blk"]
    ng = mesh.shape["group"]
    nz = ng // 4
    return jax.shard_map(
        functools.partial(local, nb, ng, nz),
        mesh=mesh,
        in_specs=(
            P(("blk", "group"), None),
            P("blk", None, None),
            P("blk", None, None),
            P(("blk", "group"), None),
            P(),
            P(),
            P(),
            P(),
            P(),
            P(),
        ),
        out_specs=(P(("blk", "group"), None), P(("blk", "group"), None)),
        check_vma=False,
    )
```

```python
import functools
import math

import jax
import jax.numpy as jnp
from jax import lax
from jax.experimental import pallas as pl
from jax.experimental.pallas import tpu as pltpu
from jax.sharding import PartitionSpec as P

HEADS = 16
IMG = 4
X_LOW, X_HIGH = 2, 2
LANES = 128
CHUNK = 384
LOSS_SCALE = 256.0
EPS = 1e-06
LOW = -1e30

F32 = jnp.float32
BF16 = jnp.bfloat16
MESH = pl.DeviceIdType.MESH


def mm(a, b):
    return lax.dot_general(a, b, (((1,), (0,)), ((), ())), preferred_element_type=F32)


def mm_nt(a, b):
    return lax.dot_general(a, b, (((1,), (1,)), ((), ())), preferred_element_type=F32)


def pieces(x, count):
    out = []
    for _ in range(count - 1):
        top = x.astype(BF16).astype(F32)
        out.append(top)
        x = x - top
    out.append(x.astype(BF16).astype(F32))
    return out


def stacked(x, count):
    return jnp.concatenate(pieces(x, count), axis=0).astype(BF16)


def small_rows(x, buf):
    for k, piece in enumerate(pieces(x, 3)):
        buf[k * IMG : (k + 1) * IMG, :] = piece
    return buf[...].astype(BF16)


def three(y):
    return y[0:IMG] + y[IMG : 2 * IMG] + y[2 * IMG : 3 * IMG]


def far(j, n):
    return (n // 2 + ((j + 1) // 2) * (2 * ((j + 1) % 2) - 1)) % n


def kernel(
    nb,
    ng,
    patches,
    owner_in,
    slot_in,
    text_in,
    probe,
    w_key,
    w_value,
    w_out,
    logit_scale,
    logit_bias,
    g_patch,
    g_text,
    owner,
    slot,
    text,
    wk,
    wv,
    wo,
    p,
    v,
    st,
    hm,
    kp3,
    kpr,
    ot,
    et,
    part_own,
    part_in,
    acc_out,
    acc_in,
    fs,
    rows16,
    pooled_buf,
    unit_line,
    u16,
    di_out,
    di_in,
    unit_all,
    u64,
    t_img,
    tf,
    t_txt,
    tt,
    td_out,
    td_in,
    pg_all,
    pgm,
    vg,
    load_sem,
    pair_send,
    pair_recv,
    tz_send,
    tz_recv,
    tx_send,
    tx_recv,
    tp_send,
    tp_recv,
    acc_send,
    acc_recv,
    uy_send,
    uy_recv,
    uz_send,
    uz_recv,
    di_send,
    di_recv,
    td_send,
    td_recv,
    pg_send,
    pg_recv,
    fw_send,
    fw_recv,
):
    nq = ng // 2
    nz = nq // X_HIGH
    nx = X_LOW * X_HIGH
    ny = nb // X_LOW
    nxy = nx * ny
    mine = nq * IMG
    rows, width = patches.shape
    chunks = width // CHUNK
    head_width = width // HEADS
    blk = lax.axis_index("blk")
    grp = lax.axis_index("group")
    core = grp % 2
    q = grp // 2
    z = q % nz
    xh = q // nz
    y = blk // X_LOW
    x = xh * X_LOW + blk % X_LOW
    xy = y * nx + x
    pending = []

    def at(x_, y_, z_, c_):
        return (y_ * X_LOW + x_ % X_LOW, ((x_ // X_LOW) * nz + z_) * 2 + c_)

    sibling = at(x, y, z, 1 - core)

    def group_peer(i):
        k = ((xh + far(i // nz, X_HIGH)) % X_HIGH) * nz + (z + far(i % nz, nz)) % nz
        return k, (blk, k * 2 + core)

    def z_peer(i):
        k = (z + far(i, nz)) % nz
        return k, at(x, y, k, core)

    def x_peer(i):
        k = (x + far(i, nx)) % nx
        return k, at(k, y, z, core)

    def y_peer(i):
        k = (y + far(i, ny)) % ny
        return k, at(x, k, z, core)

    def plane_peer(i):
        y_ = (y + far(i // nx, ny)) % ny
        x_ = (x + far(i % nx, nx)) % nx
        return y_ * nx + x_, at(x_, y_, z, core)

    def remote(src, dst, send, recv, device):
        return pltpu.make_async_remote_copy(
            src_ref=src,
            dst_ref=dst,
            send_sem=send,
            recv_sem=recv,
            device_id=device,
            device_id_type=MESH,
        )

    def each(count, act):
        def step(i, carry):
            act(i)
            return carry

        lax.fori_loop(0, count - 1, step, 0)

    def spread(peer, count, src_of, dst_of, me, send, recv):
        def act(i):
            k, device = peer(i)
            remote(src_of(k), dst_of(me), send.at[k], recv.at[me], device).start()

        each(count, act)

        def settle(i):
            k, device = peer(i)
            remote(src_of(k), src_of(k), send.at[k], recv.at[k], device).wait_send()

        pending.append(lambda: each(count, settle))

    def gather_wait(peer, count, dst_of, send, recv, then=None):
        def act(i):
            k, device = peer(count - 2 - i)
            remote(dst_of(k), dst_of(k), send.at[k], recv.at[k], device).wait_recv()
            if then is not None:
                then(k)

        each(count, act)

    def to_sibling(src, dst, n):
        copy = remote(src, dst, pair_send.at[n], pair_recv.at[n], sibling)
        copy.start()
        pending.append(copy.wait_send)

    def from_sibling(dst, n):
        remote(dst, dst, pair_send.at[n], pair_recv.at[n], sibling).wait_recv()

    barrier = pltpu.get_barrier_semaphore()

    def greet(peer):
        def act(i):
            pl.semaphore_signal(barrier, inc=1, device_id=peer(i)[1], device_id_type=MESH)

        return act

    each(nq, greet(group_peer))
    each(nxy, greet(plane_peer))
    pl.semaphore_signal(barrier, inc=1, device_id=sibling, device_id_type=MESH)

    loads = [
        pltpu.make_async_copy(src, dst, load_sem.at[n])
        for n, (src, dst) in enumerate(
            [
                (w_key, wk),
                (owner_in, owner),
                (slot_in, slot),
                (patches, p),
                (w_value, wv),
                (text_in, text),
                (w_out, wo),
            ]
        )
    ]
    for load in loads:
        load.start()

    row_i = lax.broadcasted_iota(jnp.int32, (LANES, width), 0)
    col_i = lax.broadcasted_iota(jnp.int32, (LANES, width), 1)
    first = (row_i & (HEADS - 1)) * head_width
    in_head = (col_i >= first) & (col_i < first + head_width)
    hm[...] = jnp.where(in_head & (row_i < 3 * HEADS), 1.0, 0.0).astype(BF16)
    q3 = pieces(probe[...].reshape(1, width) / math.sqrt(head_width), 3)
    band = lax.broadcasted_iota(jnp.int32, (3 * HEADS, width), 0) // HEADS
    q_rows = jnp.where(band == 0, q3[0], jnp.where(band == 1, q3[1], q3[2]))
    table = (q_rows * hm[0 : 3 * HEADS, :].astype(F32)).astype(BF16)
    loads[0].wait()
    kpt = mm_nt(table, wk[...])
    kp = kpt[0:HEADS] + kpt[HEADS : 2 * HEADS] + kpt[2 * HEADS : 3 * HEADS]
    kp_pieces = pieces(kp, 3)
    kp3[...] = jnp.concatenate(kp_pieces, axis=0).astype(BF16)
    kpr[...] = jnp.zeros_like(kpr)
    kpr[3 * HEADS : 6 * HEADS, :] = jnp.concatenate(
        [kp_pieces[0], kp_pieces[1], kp_pieces[0]], axis=0
    ).astype(BF16)
    rows16[...] = jnp.zeros_like(rows16)
    tt[...] = jnp.zeros_like(tt)

    loads[1].wait()
    loads[2].wait()
    own_owner = owner[0, pl.ds(grp, 1), :]
    code = (own_owner & 1) * mine + (own_owner >> 1) * IMG + slot[0, pl.ds(grp, 1), :]
    member = code == lax.broadcasted_iota(jnp.int32, (2 * mine, rows), 0)
    ot_f = jnp.where(member, 1.0, 0.0)
    ot[...] = ot_f.astype(BF16)

    loads[3].wait()
    s = mm_nt(kp3[...], p[...])
    scores = s[0:HEADS] + s[HEADS : 2 * HEADS] + s[2 * HEADS : 3 * HEADS]
    st[...] = scores
    lane = lax.broadcasted_iota(jnp.int32, (2 * mine, LANES), 1)
    peak = jnp.zeros((2 * mine, LANES), F32)
    for h in range(HEADS):
        top = jnp.max(jnp.where(member, scores[h : h + 1, :], LOW), axis=1, keepdims=True)
        peak = jnp.where(lane == h, top, peak)
    peak_t = jnp.transpose(peak)[0:HEADS]
    shift = mm(stacked(peak_t, 3), ot[...])
    shift = shift[0:HEADS] + shift[HEADS : 2 * HEADS] + shift[2 * HEADS : 3 * HEADS]
    e_hi, e_lo = pieces(jnp.exp(scores - shift), 2)
    blank = jnp.zeros((HEADS, rows), F32)
    e_pad = jnp.concatenate(
        [blank, e_hi, e_lo, jnp.zeros((LANES - 3 * HEADS, rows), F32)], axis=0
    )
    et[...] = jnp.transpose(e_pad).astype(BF16)
    stats = jnp.where(lane < HEADS, peak, mm(ot[...], et[...]))
    for c in range(2):
        part_own[c, :, width : width + LANES] = stats[c * mine : (c + 1) * mine]
    loads[4].wait()

    def pool(j, carry):
        cols = pl.ds(pl.multiple_of(j * CHUNK, CHUNK), CHUNK)
        value = mm(p[...], wv[:, cols])
        v[:, cols] = value
        x_hi, x_lo = pieces(mm(et[...], hm[:, cols]) * value, 2)
        total = mm(ot[...], x_hi.astype(BF16)) + mm(ot[...], x_lo.astype(BF16))
        for c in range(2):
            part_own[c, :, cols] = total[c * mine : (c + 1) * mine]
        return carry

    lax.fori_loop(0, chunks, pool, 0)
    loads[5].wait()
    t_img[(core * nx + x) * nz + z] = text[...]
    t_txt[xy] = text[...]

    pl.semaphore_wait(barrier, nq - 1 + nxy - 1 + 1)
    to_sibling(part_own.at[1 - core], part_in, 0)
    z_slab = lambda k: t_img.at[(core * nx + x) * nz + k]
    spread(z_peer, nz, lambda k: text, z_slab, z, tz_send, tz_recv)
    spread(plane_peer, nxy, lambda k: text, lambda k: t_txt.at[k], xy, tp_send, tp_recv)

    from_sibling(part_in, 0)
    lane_m = lax.broadcasted_iota(jnp.int32, (mine, LANES), 1)
    stat_a = part_own[core, :, width : width + LANES]
    stat_b = part_in[:, width : width + LANES]
    top = jnp.maximum(stat_a, stat_b)
    chip_stats = jnp.where(lane_m < HEADS, top, 0.0)
    scale = []
    for stat in (stat_a, stat_b):
        f = jnp.where(lane_m < HEADS, jnp.exp(stat - top), 0.0)
        chip_stats += stat * (pltpu.roll(f, HEADS, 1) + pltpu.roll(f, 2 * HEADS, 1))
        f_hi, f_lo = pieces(f, 2)
        scale.append((f_hi + pltpu.roll(f_lo, HEADS, 1)).astype(BF16))
    for k in range(nq):
        acc_out[k, :, width : width + LANES] = chip_stats[k * IMG : (k + 1) * IMG]
    for j in range(chunks):
        cols = slice(j * CHUNK, (j + 1) * CHUNK)
        total = (
            mm(scale[0], hm[:, cols]) * part_own[core, :, cols]
            + mm(scale[1], hm[:, cols]) * part_in[:, cols]
        )
        for k in range(nq):
            acc_out[k, :, cols] = total[k * IMG : (k + 1) * IMG]
    acc_slab = lambda k: acc_in.at[k]
    spread(group_peer, nq, lambda k: acc_out.at[k], acc_slab, q, acc_send, acc_recv)
    acc_in[q] = acc_out[q]

    gather_wait(z_peer, nz, z_slab, tz_send, tz_recv)
    x_slabs = lambda k: t_img.at[pl.ds((core * nx + k) * nz, nz)]
    spread(x_peer, nx, lambda k: x_slabs(x), x_slabs, x, tx_send, tx_recv)
    gather_wait(plane_peer, nxy, lambda k: t_txt.at[k], tp_send, tp_recv)
    for k in range(nxy):
        tt[k * IMG : (k + 1) * IMG, :] = t_txt[k].astype(F32)
    tt_b = tt[...].astype(BF16)
    tt_inv = 1.0 / jnp.sqrt(jnp.sum(tt[...] * tt[...], axis=1, keepdims=True) + EPS)
    tt_inv = jnp.transpose(jnp.broadcast_to(tt_inv, (LANES, LANES)))[0:1, :]
    gather_wait(x_peer, nx, x_slabs, tx_send, tx_recv)
    t_half = lambda c: t_img.at[pl.ds(c * nx * nz, nx * nz)]
    to_sibling(t_half(core), t_half(core), 1)
    loads[6].wait()

    gather_wait(group_peer, nq, acc_slab, acc_send, acc_recv)
    lane4 = lax.broadcasted_iota(jnp.int32, (IMG, LANES), 1)
    heads4 = lane4 < HEADS
    parts = [acc_in[k, :, width : width + LANES] for k in range(nq)]
    m = parts[0]
    for part in parts[1:]:
        m = jnp.maximum(m, part)
    factors = []
    denom = jnp.zeros((IMG, LANES), F32)
    for part in parts:
        f = jnp.exp(part - m)
        mass = pltpu.roll(part, LANES - HEADS, 1) + pltpu.roll(part, LANES - 2 * HEADS, 1)
        factors.append(f)
        denom = denom + f * mass
    denom = jnp.where(heads4, denom, 1.0)
    lse = m + jnp.log(denom)
    for k, f in enumerate(factors):
        f_hi, f_lo = pieces(jnp.where(heads4, f / denom, 0.0), 2)
        fs[k * IMG : (k + 1) * IMG, :] = f_hi + pltpu.roll(f_lo, HEADS, 1)
    factor = mm(fs[...].astype(BF16), hm[...])
    pooled = jnp.zeros((IMG, width), F32)
    for k in range(nq):
        pooled = pooled + factor[k * IMG : (k + 1) * IMG] * acc_in[k, :, 0:width]
    pooled_buf[...] = pooled
    embeds = three(mm(small_rows(pooled, rows16), wo[...]))
    norm = jnp.sqrt(jnp.sum(embeds * embeds, axis=1, keepdims=True) + EPS)
    unit = embeds / norm
    unit_line[y] = unit
    unit_all[core, z] = unit
    y_slab = lambda k: unit_line.at[k]
    spread(y_peer, ny, lambda k: unit_line.at[y], y_slab, y, uy_send, uy_recv)
    u_slab = lambda k: unit_all.at[core, k]
    spread(z_peer, nz, lambda k: unit_all.at[core, z], u_slab, z, uz_send, uz_recv)

    from_sibling(t_half(1 - core), 1)
    ntext = 2 * nx * nz * IMG
    for k in range(2 * nx * nz):
        tf[k * IMG : (k + 1) * IMG, :] = t_img[k].astype(F32)
    texts = tf[...]
    tb = texts.astype(BF16)
    inv = 1.0 / jnp.sqrt(jnp.sum(texts * texts, axis=1, keepdims=True) + EPS)
    inv_row = jnp.transpose(jnp.broadcast_to(inv, (ntext, LANES)))[0:1, :]
    temper = jnp.exp(jnp.full((1, 1), logit_scale[0], F32))

    def block_signal(u_pieces, tb_, inv_, image_slab, text_slab):
        n, t = u_pieces[0].shape[0], tb_.shape[0]
        dots = mm_nt(jnp.concatenate(u_pieces, axis=0).astype(BF16), tb_)
        dots = dots[0:n] + dots[n : 2 * n] + dots[2 * n : 3 * n]
        logits = temper * (dots * inv_) + logit_bias[0]
        row = lax.broadcasted_iota(jnp.int32, (n, t), 0)
        col = lax.broadcasted_iota(jnp.int32, (n, t), 1)
        positive = ((row >> 2) == image_slab) & (col - text_slab * IMG == (row & (IMG - 1)))
        return 1.0 / (1.0 + jnp.exp(-logits)) - jnp.where(positive, 1.0, 0.0)

    gather_wait(y_peer, ny, y_slab, uy_send, uy_recv)
    nline = ny * IMG
    for k in range(ny):
        u16[k * IMG : (k + 1) * IMG, :] = unit_line[k]
    signal = block_signal(pieces(u16[...], 3), tb, inv_row, y, (core * nx + x) * nz + z)
    di = mm(stacked(signal * inv_row, 3), tb)
    di = di[0:nline] + di[nline : 2 * nline] + di[2 * nline : 3 * nline]
    for k in range(ny):
        di_out[k] = di[k * IMG : (k + 1) * IMG]
    di_slab = lambda k: di_in.at[k]
    spread(y_peer, ny, lambda k: di_out.at[k], di_slab, y, di_send, di_recv)
    di_in[y] = di_out[y]

    gather_wait(z_peer, nz, u_slab, uz_send, uz_recv)
    to_sibling(unit_all.at[core], unit_all.at[core], 2)
    from_sibling(unit_all.at[1 - core], 2)
    for c in range(2):
        for k in range(nz):
            r = (c * nz + k) * IMG
            u64[r : r + IMG, :] = unit_all[c, k]
    u_pieces = pieces(u64[...], 3)
    s_hi, s_lo = pieces(block_signal(u_pieces, tt_b, tt_inv, core * nz + z, xy), 2)
    gap = -6 * nz * IMG % LANES
    s_pad = jnp.concatenate([s_hi, s_hi, s_lo, jnp.zeros((gap, LANES), F32)], axis=0)
    u_pad = jnp.concatenate(
        [u_pieces[0], u_pieces[1], u_pieces[0], jnp.zeros((gap, width), F32)], axis=0
    )
    td = mm(jnp.transpose(s_pad).astype(BF16), u_pad.astype(BF16))
    for k in range(nxy):
        td_out[k] = td[k * IMG : (k + 1) * IMG]
    td_slab = lambda k: td_in.at[k]
    spread(plane_peer, nxy, lambda k: td_out.at[k], td_slab, xy, td_send, td_recv)
    td_in[xy] = td_out[xy]

    gather_wait(y_peer, ny, di_slab, di_send, di_recv)
    dunit = di_in[0]
    for k in range(1, ny):
        dunit = dunit + di_in[k]
    dunit = dunit * (temper * LOSS_SCALE)
    unit = unit_line[y]
    embed_grad = (dunit - unit * jnp.sum(unit * dunit, axis=1, keepdims=True)) / norm
    pooled_grad = three(mm_nt(small_rows(embed_grad, rows16), wo[...]))
    mass = three(mm_nt(small_rows(pooled_grad * pooled_buf[...], rows16), hm[...]))
    pg_all[core, q, :, 0:width] = pooled_grad
    pg_all[core, q, :, width : width + LANES] = jnp.where(
        heads4, lse, jnp.where(lane4 < 2 * HEADS, mass, 0.0)
    )
    pg_slab = lambda k: pg_all.at[core, k]
    spread(group_peer, nq, lambda k: pg_slab(q), pg_slab, q, pg_send, pg_recv)

    def forward(k):
        remote(pg_slab(k), pg_slab(k), fw_send.at[k], fw_recv.at[k], sibling).start()

    forward(q)
    gather_wait(group_peer, nq, pg_slab, pg_send, pg_recv, forward)
    for k in range(nq):
        pgm[core, k * IMG : (k + 1) * IMG, :] = pg_all[core, k]

    gather_wait(plane_peer, nxy, td_slab, td_send, td_recv)
    text_dunit = td_in[0]
    for k in range(1, nxy):
        text_dunit = text_dunit + td_in[k]
    text_dunit = text_dunit * (temper * LOSS_SCALE)
    own_text = text[...].astype(F32)
    text_norm = jnp.sqrt(jnp.sum(own_text * own_text, axis=1, keepdims=True) + EPS)
    text_unit = own_text / text_norm
    g_text[...] = (
        (text_dunit - text_unit * jnp.sum(text_unit * text_dunit, axis=1, keepdims=True))
        / text_norm
    ).astype(BF16)

    def arrived(k, carry):
        other = pg_all.at[1 - core, k]
        remote(other, other, fw_send.at[k], fw_recv.at[k], sibling).wait_recv()
        return carry

    lax.fori_loop(0, nq, arrived, 0)
    for k in range(nq):
        pgm[1 - core, k * IMG : (k + 1) * IMG, :] = pg_all[1 - core, k]
    row_stats = jnp.concatenate([pgm[0, :, width:], pgm[1, :, width:]], axis=0)
    row_stats = mm(stacked(jnp.transpose(row_stats)[0 : 2 * HEADS], 3), ot[...])
    row_stats = (
        row_stats[0 : 2 * HEADS] + row_stats[2 * HEADS : 4 * HEADS] + row_stats[4 * HEADS : 6 * HEADS]
    )
    own_o = jnp.transpose(jnp.concatenate([ot_f, ot_f], axis=0)).astype(BF16)
    pg = jnp.concatenate([pgm[0, :, 0:width], pgm[1, :, 0:width]], axis=0)
    pgr = mm(own_o, stacked(pg, 2))
    d_hi, d_lo = pieces(pgr * v[...], 2)
    dw = mm_nt(hm[0:HEADS, :], d_hi.astype(BF16)) + mm_nt(hm[0:HEADS, :], d_lo.astype(BF16))
    w = jnp.exp(st[...] - row_stats[0:HEADS])
    ds = w * (dw - row_stats[HEADS : 2 * HEADS])
    w_hi, w_lo = pieces(w, 2)
    ds_hi, ds_lo = pieces(ds, 2)
    wt = jnp.transpose(
        jnp.concatenate([w_hi, w_lo, blank, ds_hi, ds_hi, ds_lo, blank, blank], axis=0)
    ).astype(BF16)
    vg[...] = stacked(mm(wt, hm[...]) * pgr, 2)
    et[...] = wt

    def back(j, carry):
        cols = pl.ds(pl.multiple_of(j * CHUNK, CHUNK), CHUNK)
        g = mm_nt(vg[...], wv[cols, :])
        g_patch[:, cols] = (g[0:rows] + g[rows : 2 * rows] + mm(et[...], kpr[:, cols])).astype(BF16)
        return carry

    lax.fori_loop(0, chunks, back, 0)

    def forwarded(k, carry):
        remote(pg_slab(k), pg_slab(k), fw_send.at[k], fw_recv.at[k], sibling).wait_send()
        return carry

    lax.fori_loop(0, nq, forwarded, 0)
    for settle in pending:
        settle()


def local(nb, ng, patches, owner, slot, text, probe, w_key, w_value, w_out, scale, bias):
    rows, width = patches.shape
    nq = ng // 2
    nz = nq // X_HIGH
    nx = X_LOW * X_HIGH
    ny = nb // X_LOW
    nxy = nx * ny
    mine = nq * IMG
    wide = width + LANES
    vmem = pl.BlockSpec(memory_space=pltpu.VMEM)
    smem = pl.BlockSpec(memory_space=pltpu.SMEM)
    anywhere = pl.BlockSpec(memory_space=pl.ANY)
    weight = pltpu.VMEM((width, width), BF16)
    dma = pltpu.SemaphoreType.DMA
    two = lambda n: [dma((n,)), dma((n,))]
    return pl.pallas_call(
        functools.partial(kernel, nb, ng),
        out_shape=(
            jax.ShapeDtypeStruct((rows, width), BF16),
            jax.ShapeDtypeStruct((IMG, width), BF16),
        ),
        in_specs=[anywhere] * 4 + [vmem] + [anywhere] * 3 + [smem, smem],
        out_specs=(vmem, vmem),
        scratch_shapes=[
            pltpu.VMEM(owner.shape, jnp.int32),
            pltpu.VMEM(slot.shape, jnp.int32),
            pltpu.VMEM(text.shape, BF16),
            weight,
            weight,
            weight,
            pltpu.VMEM((rows, width), BF16),
            pltpu.VMEM((rows, width), F32),
            pltpu.VMEM((HEADS, rows), F32),
            pltpu.VMEM((LANES, width), BF16),
            pltpu.VMEM((3 * HEADS, width), BF16),
            pltpu.VMEM((LANES, width), BF16),
            pltpu.VMEM((2 * mine, rows), BF16),
            pltpu.VMEM((rows, LANES), BF16),
            pltpu.VMEM((2, mine, wide), F32),
            pltpu.VMEM((mine, wide), F32),
            pltpu.VMEM((nq, IMG, wide), F32),
            pltpu.VMEM((nq, IMG, wide), F32),
            pltpu.VMEM((mine, LANES), F32),
            pltpu.VMEM((16, width), F32),
            pltpu.VMEM((IMG, width), F32),
            pltpu.VMEM((ny, IMG, width), F32),
            pltpu.VMEM((ny * IMG, width), F32),
            pltpu.VMEM((ny, IMG, width), F32),
            pltpu.VMEM((ny, IMG, width), F32),
            pltpu.VMEM((2, nz, IMG, width), F32),
            pltpu.VMEM((2 * nz * IMG, width), F32),
            pltpu.VMEM((2 * nx * nz, IMG, width), BF16),
            pltpu.VMEM((2 * nx * nz * IMG, width), F32),
            pltpu.VMEM((nxy, IMG, width), BF16),
            pltpu.VMEM((LANES, width), F32),
            pltpu.VMEM((nxy, IMG, width), F32),
            pltpu.VMEM((nxy, IMG, width), F32),
            pltpu.VMEM((2, nq, IMG, wide), F32),
            pltpu.VMEM((2, mine, wide), F32),
            pltpu.VMEM((2 * rows, width), BF16),
            dma((7,)),
            *two(3),
            *two(nz),
            *two(nx),
            *two(nxy),
            *two(nq),
            *two(ny),
            *two(nz),
            *two(ny),
            *two(nxy),
            *two(nq),
            *two(nq),
        ],
        compiler_params=pltpu.CompilerParams(
            collective_id=0, has_side_effects=True, vmem_limit_bytes=56 * 2**20
        ),
        name="pool_contrast",
    )(patches, owner, slot, text, probe, w_key, w_value, w_out, scale, bias)


def solution(mesh):
    nb = mesh.shape["blk"]
    ng = mesh.shape["group"]
    return jax.shard_map(
        functools.partial(local, nb, ng),
        mesh=mesh,
        in_specs=(
            P(("blk", "group"), None),
            P("blk", None, None),
            P("blk", None, None),
            P(("blk", "group"), None),
            P(),
            P(),
            P(),
            P(),
            P(),
            P(),
        ),
        out_specs=(P(("blk", "group"), None), P(("blk", "group"), None)),
        check_vma=False,
    )
```

```python
import functools
import math

import jax
import jax.numpy as jnp
from jax import lax
from jax.experimental import pallas as pl
from jax.experimental.pallas import tpu as pltpu
from jax.sharding import PartitionSpec as P

HEADS = 16
IMG = 4
X_LOW, X_HIGH = 2, 2
LANES = 128
CHUNK = 384
LOSS_SCALE = 256.0
EPS = 1e-06
LOW = -1e30

F32 = jnp.float32
BF16 = jnp.bfloat16
MESH = pl.DeviceIdType.MESH


def mm(a, b):
    return lax.dot_general(a, b, (((1,), (0,)), ((), ())), preferred_element_type=F32)


def mm_nt(a, b):
    return lax.dot_general(a, b, (((1,), (1,)), ((), ())), preferred_element_type=F32)


def pieces(x, count):
    out = []
    for _ in range(count - 1):
        top = x.astype(BF16).astype(F32)
        out.append(top)
        x = x - top
    out.append(x.astype(BF16).astype(F32))
    return out


def stacked(x, count):
    return jnp.concatenate(pieces(x, count), axis=0).astype(BF16)


def small_rows(x, buf):
    for k, piece in enumerate(pieces(x, 3)):
        buf[k * IMG : (k + 1) * IMG, :] = piece
    return buf[...].astype(BF16)


def three(y):
    return y[0:IMG] + y[IMG : 2 * IMG] + y[2 * IMG : 3 * IMG]


def far(j, n):
    return (n // 2 + ((j + 1) // 2) * (2 * ((j + 1) % 2) - 1)) % n


def kernel(
    nb,
    ng,
    patches,
    owner_in,
    slot_in,
    text_in,
    probe,
    w_key,
    w_value,
    w_out,
    logit_scale,
    logit_bias,
    g_patch,
    g_text,
    owner,
    slot,
    text,
    wk,
    wv,
    wo,
    p,
    v,
    st,
    hm,
    kp3,
    kpr,
    ot,
    et,
    part_own,
    part_in,
    acc_out,
    acc_in,
    fs,
    rows16,
    pooled_buf,
    unit_line,
    u16,
    di_out,
    di_in,
    unit_all,
    u64,
    t_img,
    tf,
    t_txt,
    tt,
    td_out,
    td_in,
    pg_all,
    pgm,
    vg,
    load_sem,
    pair_send,
    pair_recv,
    tz_send,
    tz_recv,
    tx_send,
    tx_recv,
    tp_send,
    tp_recv,
    acc_send,
    acc_recv,
    uy_send,
    uy_recv,
    uz_send,
    uz_recv,
    di_send,
    di_recv,
    td_send,
    td_recv,
    pg_send,
    pg_recv,
    fw_send,
    fw_recv,
):
    nq = ng // 2
    nz = nq // X_HIGH
    nx = X_LOW * X_HIGH
    ny = nb // X_LOW
    nxy = nx * ny
    mine = nq * IMG
    rows, width = patches.shape
    chunks = width // CHUNK
    head_width = width // HEADS
    blk = lax.axis_index("blk")
    grp = lax.axis_index("group")
    core = grp % 2
    q = grp // 2
    z = q % nz
    xh = q // nz
    y = blk // X_LOW
    x = xh * X_LOW + blk % X_LOW
    xy = y * nx + x
    pending = []

    def at(x_, y_, z_, c_):
        return (y_ * X_LOW + x_ % X_LOW, ((x_ // X_LOW) * nz + z_) * 2 + c_)

    sibling = at(x, y, z, 1 - core)

    def group_peer(i):
        k = ((xh + far(i // nz, X_HIGH)) % X_HIGH) * nz + (z + far(i % nz, nz)) % nz
        return k, (blk, k * 2 + core)

    def z_peer(i):
        k = (z + far(i, nz)) % nz
        return k, at(x, y, k, core)

    def x_peer(i):
        k = (x + far(i, nx)) % nx
        return k, at(k, y, z, core)

    def y_peer(i):
        k = (y + far(i, ny)) % ny
        return k, at(x, k, z, core)

    def plane_peer(i):
        y_ = (y + far(i // nx, ny)) % ny
        x_ = (x + far(i % nx, nx)) % nx
        return y_ * nx + x_, at(x_, y_, z, core)

    def remote(src, dst, send, recv, device):
        return pltpu.make_async_remote_copy(
            src_ref=src,
            dst_ref=dst,
            send_sem=send,
            recv_sem=recv,
            device_id=device,
            device_id_type=MESH,
        )

    def each(count, act):
        def step(i, carry):
            act(i)
            return carry

        lax.fori_loop(0, count - 1, step, 0)

    def spread(peer, count, src_of, dst_of, me, send, recv):
        def act(i):
            k, device = peer(i)
            remote(src_of(k), dst_of(me), send.at[k], recv.at[me], device).start()

        each(count, act)

        def settle(i):
            k, device = peer(i)
            remote(src_of(k), src_of(k), send.at[k], recv.at[k], device).wait_send()

        pending.append(lambda: each(count, settle))

    def gather_wait(peer, count, dst_of, send, recv, then=None):
        def act(i):
            k, device = peer(count - 2 - i)
            remote(dst_of(k), dst_of(k), send.at[k], recv.at[k], device).wait_recv()
            if then is not None:
                then(k)

        each(count, act)

    def to_sibling(src, dst, n):
        copy = remote(src, dst, pair_send.at[n], pair_recv.at[n], sibling)
        copy.start()
        pending.append(copy.wait_send)

    def from_sibling(dst, n):
        remote(dst, dst, pair_send.at[n], pair_recv.at[n], sibling).wait_recv()

    barrier = pltpu.get_barrier_semaphore()

    def greet(peer):
        def act(i):
            pl.semaphore_signal(barrier, inc=1, device_id=peer(i)[1], device_id_type=MESH)

        return act

    each(nq, greet(group_peer))
    each(nxy, greet(plane_peer))
    pl.semaphore_signal(barrier, inc=1, device_id=sibling, device_id_type=MESH)

    loads = [
        pltpu.make_async_copy(src, dst, load_sem.at[n])
        for n, (src, dst) in enumerate(
            [
                (w_key, wk),
                (owner_in, owner),
                (slot_in, slot),
                (patches, p),
                (w_value, wv),
                (text_in, text),
                (w_out, wo),
            ]
        )
    ]
    for load in loads:
        load.start()

    row_i = lax.broadcasted_iota(jnp.int32, (LANES, width), 0)
    col_i = lax.broadcasted_iota(jnp.int32, (LANES, width), 1)
    first = (row_i & (HEADS - 1)) * head_width
    in_head = (col_i >= first) & (col_i < first + head_width)
    hm[...] = jnp.where(in_head & (row_i < 3 * HEADS), 1.0, 0.0).astype(BF16)
    q3 = pieces(probe[...].reshape(1, width) / math.sqrt(head_width), 3)
    band = lax.broadcasted_iota(jnp.int32, (3 * HEADS, width), 0) // HEADS
    q_rows = jnp.where(band == 0, q3[0], jnp.where(band == 1, q3[1], q3[2]))
    table = (q_rows * hm[0 : 3 * HEADS, :].astype(F32)).astype(BF16)
    loads[0].wait()
    kpt = mm_nt(table, wk[...])
    kp = kpt[0:HEADS] + kpt[HEADS : 2 * HEADS] + kpt[2 * HEADS : 3 * HEADS]
    kp_pieces = pieces(kp, 3)
    kp3[...] = jnp.concatenate(kp_pieces, axis=0).astype(BF16)
    kpr[...] = jnp.zeros_like(kpr)
    kpr[3 * HEADS : 6 * HEADS, :] = jnp.concatenate(
        [kp_pieces[0], kp_pieces[1], kp_pieces[0]], axis=0
    ).astype(BF16)
    rows16[...] = jnp.zeros_like(rows16)
    tt[...] = jnp.zeros_like(tt)

    loads[1].wait()
    loads[2].wait()
    own_owner = owner[0, pl.ds(grp, 1), :]
    code = (own_owner & 1) * mine + (own_owner >> 1) * IMG + slot[0, pl.ds(grp, 1), :]
    member = code == lax.broadcasted_iota(jnp.int32, (2 * mine, rows), 0)
    ot_f = jnp.where(member, 1.0, 0.0)
    ot[...] = ot_f.astype(BF16)

    loads[3].wait()
    s = mm_nt(kp3[...], p[...])
    scores = s[0:HEADS] + s[HEADS : 2 * HEADS] + s[2 * HEADS : 3 * HEADS]
    st[...] = scores
    lane = lax.broadcasted_iota(jnp.int32, (2 * mine, LANES), 1)
    peak = jnp.zeros((2 * mine, LANES), F32)
    for h in range(HEADS):
        top = jnp.max(jnp.where(member, scores[h : h + 1, :], LOW), axis=1, keepdims=True)
        peak = jnp.where(lane == h, top, peak)
    peak_t = jnp.transpose(peak)[0:HEADS]
    shift = mm(stacked(peak_t, 3), ot[...])
    shift = shift[0:HEADS] + shift[HEADS : 2 * HEADS] + shift[2 * HEADS : 3 * HEADS]
    e_hi, e_lo = pieces(jnp.exp(scores - shift), 2)
    blank = jnp.zeros((HEADS, rows), F32)
    e_pad = jnp.concatenate(
        [blank, e_hi, e_lo, jnp.zeros((LANES - 3 * HEADS, rows), F32)], axis=0
    )
    et[...] = jnp.transpose(e_pad).astype(BF16)
    stats = jnp.where(lane < HEADS, peak, mm(ot[...], et[...]))
    for c in range(2):
        part_own[c, :, width : width + LANES] = stats[c * mine : (c + 1) * mine]
    loads[4].wait()

    def pool(j, carry):
        cols = pl.ds(pl.multiple_of(j * CHUNK, CHUNK), CHUNK)
        value = mm(p[...], wv[:, cols])
        v[:, cols] = value
        x_hi, x_lo = pieces(mm(et[...], hm[:, cols]) * value, 2)
        total = mm(ot[...], x_hi.astype(BF16)) + mm(ot[...], x_lo.astype(BF16))
        for c in range(2):
            part_own[c, :, cols] = total[c * mine : (c + 1) * mine]
        return carry

    lax.fori_loop(0, chunks, pool, 0)
    loads[5].wait()
    t_img[(core * nx + x) * nz + z] = text[...]
    t_txt[xy] = text[...]

    pl.semaphore_wait(barrier, nq - 1 + nxy - 1 + 1)
    to_sibling(part_own.at[1 - core], part_in, 0)

    from_sibling(part_in, 0)
    lane_m = lax.broadcasted_iota(jnp.int32, (mine, LANES), 1)
    stat_a = part_own[core, :, width : width + LANES]
    stat_b = part_in[:, width : width + LANES]
    top = jnp.maximum(stat_a, stat_b)
    chip_stats = jnp.where(lane_m < HEADS, top, 0.0)
    scale = []
    for stat in (stat_a, stat_b):
        f = jnp.where(lane_m < HEADS, jnp.exp(stat - top), 0.0)
        chip_stats += stat * (pltpu.roll(f, HEADS, 1) + pltpu.roll(f, 2 * HEADS, 1))
        f_hi, f_lo = pieces(f, 2)
        scale.append((f_hi + pltpu.roll(f_lo, HEADS, 1)).astype(BF16))
    for k in range(nq):
        acc_out[k, :, width : width + LANES] = chip_stats[k * IMG : (k + 1) * IMG]
    for j in range(chunks):
        cols = slice(j * CHUNK, (j + 1) * CHUNK)
        total = (
            mm(scale[0], hm[:, cols]) * part_own[core, :, cols]
            + mm(scale[1], hm[:, cols]) * part_in[:, cols]
        )
        for k in range(nq):
            acc_out[k, :, cols] = total[k * IMG : (k + 1) * IMG]
    acc_slab = lambda k: acc_in.at[k]
    spread(group_peer, nq, lambda k: acc_out.at[k], acc_slab, q, acc_send, acc_recv)
    z_slab = lambda k: t_img.at[(core * nx + x) * nz + k]
    spread(z_peer, nz, lambda k: text, z_slab, z, tz_send, tz_recv)
    spread(plane_peer, nxy, lambda k: text, lambda k: t_txt.at[k], xy, tp_send, tp_recv)
    acc_in[q] = acc_out[q]
    gather_wait(z_peer, nz, z_slab, tz_send, tz_recv)
    x_slabs = lambda k: t_img.at[pl.ds((core * nx + k) * nz, nz)]
    spread(x_peer, nx, lambda k: x_slabs(x), x_slabs, x, tx_send, tx_recv)
    gather_wait(plane_peer, nxy, lambda k: t_txt.at[k], tp_send, tp_recv)
    for k in range(nxy):
        tt[k * IMG : (k + 1) * IMG, :] = t_txt[k].astype(F32)
    tt_b = tt[...].astype(BF16)
    tt_inv = 1.0 / jnp.sqrt(jnp.sum(tt[...] * tt[...], axis=1, keepdims=True) + EPS)
    tt_inv = jnp.transpose(jnp.broadcast_to(tt_inv, (LANES, LANES)))[0:1, :]
    gather_wait(x_peer, nx, x_slabs, tx_send, tx_recv)
    t_half = lambda c: t_img.at[pl.ds(c * nx * nz, nx * nz)]
    to_sibling(t_half(core), t_half(core), 1)
    loads[6].wait()

    gather_wait(group_peer, nq, acc_slab, acc_send, acc_recv)
    lane4 = lax.broadcasted_iota(jnp.int32, (IMG, LANES), 1)
    heads4 = lane4 < HEADS
    parts = [acc_in[k, :, width : width + LANES] for k in range(nq)]
    m = parts[0]
    for part in parts[1:]:
        m = jnp.maximum(m, part)
    factors = []
    denom = jnp.zeros((IMG, LANES), F32)
    for part in parts:
        f = jnp.exp(part - m)
        mass = pltpu.roll(part, LANES - HEADS, 1) + pltpu.roll(part, LANES - 2 * HEADS, 1)
        factors.append(f)
        denom = denom + f * mass
    denom = jnp.where(heads4, denom, 1.0)
    lse = m + jnp.log(denom)
    for k, f in enumerate(factors):
        f_hi, f_lo = pieces(jnp.where(heads4, f / denom, 0.0), 2)
        fs[k * IMG : (k + 1) * IMG, :] = f_hi + pltpu.roll(f_lo, HEADS, 1)
    factor = mm(fs[...].astype(BF16), hm[...])
    pooled = jnp.zeros((IMG, width), F32)
    for k in range(nq):
        pooled = pooled + factor[k * IMG : (k + 1) * IMG] * acc_in[k, :, 0:width]
    pooled_buf[...] = pooled
    embeds = three(mm(small_rows(pooled, rows16), wo[...]))
    norm = jnp.sqrt(jnp.sum(embeds * embeds, axis=1, keepdims=True) + EPS)
    unit = embeds / norm
    unit_line[y] = unit
    unit_all[core, z] = unit
    y_slab = lambda k: unit_line.at[k]
    spread(y_peer, ny, lambda k: unit_line.at[y], y_slab, y, uy_send, uy_recv)
    u_slab = lambda k: unit_all.at[core, k]
    spread(z_peer, nz, lambda k: unit_all.at[core, z], u_slab, z, uz_send, uz_recv)

    from_sibling(t_half(1 - core), 1)
    ntext = 2 * nx * nz * IMG
    for k in range(2 * nx * nz):
        tf[k * IMG : (k + 1) * IMG, :] = t_img[k].astype(F32)
    texts = tf[...]
    tb = texts.astype(BF16)
    inv = 1.0 / jnp.sqrt(jnp.sum(texts * texts, axis=1, keepdims=True) + EPS)
    inv_row = jnp.transpose(jnp.broadcast_to(inv, (ntext, LANES)))[0:1, :]
    temper = jnp.exp(jnp.full((1, 1), logit_scale[0], F32))

    def block_signal(u_pieces, tb_, inv_, image_slab, text_slab):
        n, t = u_pieces[0].shape[0], tb_.shape[0]
        dots = mm_nt(jnp.concatenate(u_pieces, axis=0).astype(BF16), tb_)
        dots = dots[0:n] + dots[n : 2 * n] + dots[2 * n : 3 * n]
        logits = temper * (dots * inv_) + logit_bias[0]
        row = lax.broadcasted_iota(jnp.int32, (n, t), 0)
        col = lax.broadcasted_iota(jnp.int32, (n, t), 1)
        positive = ((row >> 2) == image_slab) & (col - text_slab * IMG == (row & (IMG - 1)))
        return 1.0 / (1.0 + jnp.exp(-logits)) - jnp.where(positive, 1.0, 0.0)

    gather_wait(y_peer, ny, y_slab, uy_send, uy_recv)
    nline = ny * IMG
    for k in range(ny):
        u16[k * IMG : (k + 1) * IMG, :] = unit_line[k]
    signal = block_signal(pieces(u16[...], 3), tb, inv_row, y, (core * nx + x) * nz + z)
    di = mm(stacked(signal * inv_row, 3), tb)
    di = di[0:nline] + di[nline : 2 * nline] + di[2 * nline : 3 * nline]
    for k in range(ny):
        di_out[k] = di[k * IMG : (k + 1) * IMG]
    di_slab = lambda k: di_in.at[k]
    spread(y_peer, ny, lambda k: di_out.at[k], di_slab, y, di_send, di_recv)
    di_in[y] = di_out[y]

    gather_wait(y_peer, ny, di_slab, di_send, di_recv)
    dunit = di_in[0]
    for k in range(1, ny):
        dunit = dunit + di_in[k]
    dunit = dunit * (temper * LOSS_SCALE)
    unit = unit_line[y]
    embed_grad = (dunit - unit * jnp.sum(unit * dunit, axis=1, keepdims=True)) / norm
    pooled_grad = three(mm_nt(small_rows(embed_grad, rows16), wo[...]))
    mass = three(mm_nt(small_rows(pooled_grad * pooled_buf[...], rows16), hm[...]))
    pg_all[core, q, :, 0:width] = pooled_grad
    pg_all[core, q, :, width : width + LANES] = jnp.where(
        heads4, lse, jnp.where(lane4 < 2 * HEADS, mass, 0.0)
    )
    pg_slab = lambda k: pg_all.at[core, k]
    spread(group_peer, nq, lambda k: pg_slab(q), pg_slab, q, pg_send, pg_recv)

    def forward(k):
        remote(pg_slab(k), pg_slab(k), fw_send.at[k], fw_recv.at[k], sibling).start()

    forward(q)

    gather_wait(z_peer, nz, u_slab, uz_send, uz_recv)
    to_sibling(unit_all.at[core], unit_all.at[core], 2)
    from_sibling(unit_all.at[1 - core], 2)
    for c in range(2):
        for k in range(nz):
            r = (c * nz + k) * IMG
            u64[r : r + IMG, :] = unit_all[c, k]
    u_pieces = pieces(u64[...], 3)
    s_hi, s_lo = pieces(block_signal(u_pieces, tt_b, tt_inv, core * nz + z, xy), 2)
    gap = -6 * nz * IMG % LANES
    s_pad = jnp.concatenate([s_hi, s_hi, s_lo, jnp.zeros((gap, LANES), F32)], axis=0)
    u_pad = jnp.concatenate(
        [u_pieces[0], u_pieces[1], u_pieces[0], jnp.zeros((gap, width), F32)], axis=0
    )
    td = mm(jnp.transpose(s_pad).astype(BF16), u_pad.astype(BF16))
    for k in range(nxy):
        td_out[k] = td[k * IMG : (k + 1) * IMG]
    td_slab = lambda k: td_in.at[k]
    spread(plane_peer, nxy, lambda k: td_out.at[k], td_slab, xy, td_send, td_recv)
    td_in[xy] = td_out[xy]

    gather_wait(group_peer, nq, pg_slab, pg_send, pg_recv, forward)
    for k in range(nq):
        pgm[core, k * IMG : (k + 1) * IMG, :] = pg_all[core, k]

    def arrived(k, carry):
        other = pg_all.at[1 - core, k]
        remote(other, other, fw_send.at[k], fw_recv.at[k], sibling).wait_recv()
        return carry

    lax.fori_loop(0, nq, arrived, 0)
    for k in range(nq):
        pgm[1 - core, k * IMG : (k + 1) * IMG, :] = pg_all[1 - core, k]
    row_stats = jnp.concatenate([pgm[0, :, width:], pgm[1, :, width:]], axis=0)
    row_stats = mm(stacked(jnp.transpose(row_stats)[0 : 2 * HEADS], 3), ot[...])
    row_stats = (
        row_stats[0 : 2 * HEADS] + row_stats[2 * HEADS : 4 * HEADS] + row_stats[4 * HEADS : 6 * HEADS]
    )
    own_o = jnp.transpose(jnp.concatenate([ot_f, ot_f], axis=0)).astype(BF16)
    pg = jnp.concatenate([pgm[0, :, 0:width], pgm[1, :, 0:width]], axis=0)
    pgr = mm(own_o, stacked(pg, 2))
    d_hi, d_lo = pieces(pgr * v[...], 2)
    dw = mm_nt(hm[0:HEADS, :], d_hi.astype(BF16)) + mm_nt(hm[0:HEADS, :], d_lo.astype(BF16))
    w = jnp.exp(st[...] - row_stats[0:HEADS])
    ds = w * (dw - row_stats[HEADS : 2 * HEADS])
    w_hi, w_lo = pieces(w, 2)
    ds_hi, ds_lo = pieces(ds, 2)
    wt = jnp.transpose(
        jnp.concatenate([w_hi, w_lo, blank, ds_hi, ds_hi, ds_lo, blank, blank], axis=0)
    ).astype(BF16)
    vg[...] = stacked(mm(wt, hm[...]) * pgr, 2)
    et[...] = wt

    def back(j, carry):
        cols = pl.ds(pl.multiple_of(j * CHUNK, CHUNK), CHUNK)
        g = mm_nt(vg[...], wv[cols, :])
        g_patch[:, cols] = (g[0:rows] + g[rows : 2 * rows] + mm(et[...], kpr[:, cols])).astype(BF16)
        return carry

    lax.fori_loop(0, chunks, back, 0)

    gather_wait(plane_peer, nxy, td_slab, td_send, td_recv)
    text_dunit = td_in[0]
    for k in range(1, nxy):
        text_dunit = text_dunit + td_in[k]
    text_dunit = text_dunit * (temper * LOSS_SCALE)
    own_text = text[...].astype(F32)
    text_norm = jnp.sqrt(jnp.sum(own_text * own_text, axis=1, keepdims=True) + EPS)
    text_unit = own_text / text_norm
    g_text[...] = (
        (text_dunit - text_unit * jnp.sum(text_unit * text_dunit, axis=1, keepdims=True))
        / text_norm
    ).astype(BF16)

    def forwarded(k, carry):
        remote(pg_slab(k), pg_slab(k), fw_send.at[k], fw_recv.at[k], sibling).wait_send()
        return carry

    lax.fori_loop(0, nq, forwarded, 0)
    for settle in pending:
        settle()


def hand_over(patch_in, text_in, patch_out, text_out, sem):
    copies = [
        pltpu.make_async_copy(patch_in, patch_out, sem.at[0]),
        pltpu.make_async_copy(text_in, text_out, sem.at[1]),
    ]
    for copy in copies:
        copy.start()
    for copy in copies:
        copy.wait()


def local(nb, ng, patches, owner, slot, text, probe, w_key, w_value, w_out, scale, bias):
    rows, width = patches.shape
    nq = ng // 2
    nz = nq // X_HIGH
    nx = X_LOW * X_HIGH
    ny = nb // X_LOW
    nxy = nx * ny
    mine = nq * IMG
    wide = width + LANES
    vmem = pl.BlockSpec(memory_space=pltpu.VMEM)
    anywhere = pl.BlockSpec(memory_space=pl.ANY)
    smem = pl.BlockSpec(memory_space=pltpu.SMEM)
    weight = pltpu.VMEM((width, width), BF16)
    dma = pltpu.SemaphoreType.DMA
    two = lambda n: [dma((n,)), dma((n,))]
    shapes = (
        jax.ShapeDtypeStruct((rows, width), BF16),
        jax.ShapeDtypeStruct((IMG, width), BF16),
    )
    grads = pl.pallas_call(
        functools.partial(kernel, nb, ng),
        out_shape=shapes,
        in_specs=[anywhere] * 4 + [vmem] + [anywhere] * 3 + [smem, smem],
        out_specs=(vmem, vmem),
        scratch_shapes=[
            pltpu.VMEM(owner.shape, jnp.int32),
            pltpu.VMEM(slot.shape, jnp.int32),
            pltpu.VMEM(text.shape, BF16),
            weight,
            weight,
            weight,
            pltpu.VMEM((rows, width), BF16),
            pltpu.VMEM((rows, width), F32),
            pltpu.VMEM((HEADS, rows), F32),
            pltpu.VMEM((LANES, width), BF16),
            pltpu.VMEM((3 * HEADS, width), BF16),
            pltpu.VMEM((LANES, width), BF16),
            pltpu.VMEM((2 * mine, rows), BF16),
            pltpu.VMEM((rows, LANES), BF16),
            pltpu.VMEM((2, mine, wide), F32),
            pltpu.VMEM((mine, wide), F32),
            pltpu.VMEM((nq, IMG, wide), F32),
            pltpu.VMEM((nq, IMG, wide), F32),
            pltpu.VMEM((mine, LANES), F32),
            pltpu.VMEM((16, width), F32),
            pltpu.VMEM((IMG, width), F32),
            pltpu.VMEM((ny, IMG, width), F32),
            pltpu.VMEM((ny * IMG, width), F32),
            pltpu.VMEM((ny, IMG, width), F32),
            pltpu.VMEM((ny, IMG, width), F32),
            pltpu.VMEM((2, nz, IMG, width), F32),
            pltpu.VMEM((2 * nz * IMG, width), F32),
            pltpu.VMEM((2 * nx * nz, IMG, width), BF16),
            pltpu.VMEM((2 * nx * nz * IMG, width), F32),
            pltpu.VMEM((nxy, IMG, width), BF16),
            pltpu.VMEM((LANES, width), F32),
            pltpu.VMEM((nxy, IMG, width), F32),
            pltpu.VMEM((nxy, IMG, width), F32),
            pltpu.VMEM((2, nq, IMG, wide), F32),
            pltpu.VMEM((2, mine, wide), F32),
            pltpu.VMEM((2 * rows, width), BF16),
            dma((7,)),
            *two(3),
            *two(nz),
            *two(nx),
            *two(nxy),
            *two(nq),
            *two(ny),
            *two(nz),
            *two(ny),
            *two(nxy),
            *two(nq),
            *two(nq),
        ],
        compiler_params=pltpu.CompilerParams(
            collective_id=0, has_side_effects=True, vmem_limit_bytes=56 * 2**20
        ),
        name="pool_contrast",
    )(patches, owner, slot, text, probe, w_key, w_value, w_out, scale, bias)
    return pl.pallas_call(
        hand_over,
        out_shape=shapes,
        in_specs=[anywhere, anywhere],
        out_specs=(anywhere, anywhere),
        scratch_shapes=[dma((2,))],
        compiler_params=pltpu.CompilerParams(vmem_limit_bytes=56 * 2**20),
        name="hand_over",
    )(*grads)


def solution(mesh):
    nb = mesh.shape["blk"]
    ng = mesh.shape["group"]
    return jax.shard_map(
        functools.partial(local, nb, ng),
        mesh=mesh,
        in_specs=(
            P(("blk", "group"), None),
            P("blk", None, None),
            P("blk", None, None),
            P(("blk", "group"), None),
            P(),
            P(),
            P(),
            P(),
            P(),
            P(),
        ),
        out_specs=(P(("blk", "group"), None), P(("blk", "group"), None)),
        check_vma=False,
    )
```

```python
import functools
import math

import jax
import jax.numpy as jnp
from jax import lax
from jax.experimental import pallas as pl
from jax.experimental.pallas import tpu as pltpu
from jax.sharding import PartitionSpec as P

HEADS = 16
IMG = 4
X_LOW, X_HIGH = 2, 2
LANES = 128
CHUNK = 384
LOSS_SCALE = 256.0
EPS = 1e-06
LOW = -1e30

F32 = jnp.float32
BF16 = jnp.bfloat16
MESH = pl.DeviceIdType.MESH


def mm(a, b):
    return lax.dot_general(a, b, (((1,), (0,)), ((), ())), preferred_element_type=F32)


def mm_nt(a, b):
    return lax.dot_general(a, b, (((1,), (1,)), ((), ())), preferred_element_type=F32)


def pieces(x, count):
    out = []
    for _ in range(count - 1):
        top = x.astype(BF16).astype(F32)
        out.append(top)
        x = x - top
    out.append(x.astype(BF16).astype(F32))
    return out


def stacked(x, count):
    return jnp.concatenate(pieces(x, count), axis=0).astype(BF16)


def small_rows(x, buf):
    for k, piece in enumerate(pieces(x, 3)):
        buf[k * IMG : (k + 1) * IMG, :] = piece
    return buf[...].astype(BF16)


def three(y):
    return y[0:IMG] + y[IMG : 2 * IMG] + y[2 * IMG : 3 * IMG]


def far(n):
    return [(n // 2 + ((j + 1) // 2) * (2 * ((j + 1) % 2) - 1)) % n for j in range(n)]


def kernel(
    nb,
    ng,
    patches,
    owner_in,
    slot_in,
    text_in,
    probe,
    w_key,
    w_value,
    w_out,
    logit_scale,
    logit_bias,
    g_patch,
    g_text,
    owner,
    slot,
    text,
    wk,
    wv,
    wo,
    p,
    v,
    st,
    hm,
    kp3,
    kpr,
    ot,
    et,
    part_own,
    part_in,
    acc_out,
    acc_in,
    fs,
    rows16,
    pooled_buf,
    unit_plane,
    u16,
    di_out,
    di_in,
    u64,
    t_img,
    tf,
    tt,
    td_out,
    td_mid,
    td_in,
    pg_all,
    pgm,
    vg,
    out,
    load_sem,
    send_sem,
    recv_sem,
):
    nq = ng // 2
    nz = nq // X_HIGH
    nx = X_LOW * X_HIGH
    ny = nb // X_LOW
    nxy = nx * ny
    mine = nq * IMG
    rows, width = patches.shape
    chunks = width // CHUNK
    head_width = width // HEADS
    blk = lax.axis_index("blk")
    grp = lax.axis_index("group")
    core = lax.rem(grp, 2)
    q = lax.div(grp, 2)
    z = lax.rem(q, nz)
    xh = lax.div(q, nz)
    y = lax.div(blk, X_LOW)
    x = xh * X_LOW + lax.rem(blk, X_LOW)
    xy = y * nx + x
    pending = []

    def at(x_, y_, z_, c_):
        x_high = lax.div(x_, X_LOW)
        return (y_ * X_LOW + x_ - x_high * X_LOW, (x_high * nz + z_) * 2 + c_)

    def ring(pos, n):
        return [pos if d == 0 else lax.rem(pos + d, n) for d in far(n)]

    sibling = at(x, y, z, 1 - core)
    ring_x, ring_y, ring_z = ring(x, nx), ring(y, ny), ring(z, nz)
    z_peers = [(k, at(x, y, k, core)) for k in ring_z[:-1]]
    x_peers = [(k, at(k, y, z, core)) for k in ring_x[:-1]]
    y_peers = [(k, at(x, k, z, core)) for k in ring_y[:-1]]
    rest_peers = [(j * nx + k, at(k, j, z, core)) for k in ring_x[:-1] for j in ring_y]
    far_peers = [
        (h * nz + k, (blk, (h * nz + k) * 2 + core)) for h in ring(xh, X_HIGH)[:-1] for k in ring_z
    ]
    near_peers = [(xh * nz + k, device) for k, device in z_peers]

    def remote(src, dst, n, device):
        return pltpu.make_async_remote_copy(
            src_ref=src,
            dst_ref=dst,
            send_sem=send_sem.at[n],
            recv_sem=recv_sem.at[n],
            device_id=device,
            device_id_type=MESH,
        )

    def spread(peers, src_of, dst, n, whole):
        for k, device in peers:
            remote(src_of(k), dst, n, device).start()
        pending.append((whole, n))

    def arrived(whole, n):
        remote(whole, whole, n, sibling).wait_recv()

    def to_sibling(src, dst, n):
        spread([(0, sibling)], lambda k: src, dst, n, src)

    barrier = pltpu.get_barrier_semaphore()

    greeted = far_peers + near_peers + rest_peers + y_peers + [(0, sibling)]
    for _, device in greeted:
        pl.semaphore_signal(barrier, inc=1, device_id=device, device_id_type=MESH)

    loads = [
        pltpu.make_async_copy(src, dst, load_sem.at[n])
        for n, (src, dst) in enumerate(
            [
                (w_key, wk),
                (owner_in, owner),
                (slot_in, slot),
                (patches, p),
                (w_value, wv),
                (text_in, text),
                (w_out, wo),
            ]
        )
    ]
    for load in loads:
        load.start()

    row_i = lax.broadcasted_iota(jnp.int32, (LANES, width), 0)
    col_i = lax.broadcasted_iota(jnp.int32, (LANES, width), 1)
    first = (row_i & (HEADS - 1)) * head_width
    in_head = (col_i >= first) & (col_i < first + head_width)
    hm[...] = jnp.where(in_head & (row_i < 3 * HEADS), 1.0, 0.0).astype(BF16)
    q3 = pieces(probe[...].reshape(1, width) / math.sqrt(head_width), 3)
    band = lax.broadcasted_iota(jnp.int32, (3 * HEADS, width), 0) // HEADS
    q_rows = jnp.where(band == 0, q3[0], jnp.where(band == 1, q3[1], q3[2]))
    table = (q_rows * hm[0 : 3 * HEADS, :].astype(F32)).astype(BF16)
    loads[0].wait()
    kpt = mm_nt(table, wk[...])
    kp = kpt[0:HEADS] + kpt[HEADS : 2 * HEADS] + kpt[2 * HEADS : 3 * HEADS]
    kp_pieces = pieces(kp, 3)
    kp3[...] = jnp.concatenate(kp_pieces, axis=0).astype(BF16)
    kpr[...] = jnp.zeros_like(kpr)
    kpr[3 * HEADS : 6 * HEADS, :] = jnp.concatenate(
        [kp_pieces[0], kp_pieces[1], kp_pieces[0]], axis=0
    ).astype(BF16)
    rows16[...] = jnp.zeros_like(rows16)
    tt[...] = jnp.zeros_like(tt)

    loads[1].wait()
    loads[2].wait()
    own_owner = owner[0, pl.ds(grp, 1), :]
    code = (own_owner & 1) * mine + (own_owner >> 1) * IMG + slot[0, pl.ds(grp, 1), :]
    member = code == lax.broadcasted_iota(jnp.int32, (2 * mine, rows), 0)
    ot_f = jnp.where(member, 1.0, 0.0)
    ot[...] = ot_f.astype(BF16)

    loads[3].wait()
    s = mm_nt(kp3[...], p[...])
    scores = s[0:HEADS] + s[HEADS : 2 * HEADS] + s[2 * HEADS : 3 * HEADS]
    st[...] = scores
    lane = lax.broadcasted_iota(jnp.int32, (2 * mine, LANES), 1)
    peak = jnp.zeros((2 * mine, LANES), F32)
    for h in range(HEADS):
        top = jnp.max(jnp.where(member, scores[h : h + 1, :], LOW), axis=1, keepdims=True)
        peak = jnp.where(lane == h, top, peak)
    peak_t = jnp.transpose(peak)[0:HEADS]
    shift = mm(stacked(peak_t, 3), ot[...])
    shift = shift[0:HEADS] + shift[HEADS : 2 * HEADS] + shift[2 * HEADS : 3 * HEADS]
    e_hi, e_lo = pieces(jnp.exp(scores - shift), 2)
    blank = jnp.zeros((HEADS, rows), F32)
    e_pad = jnp.concatenate(
        [blank, e_hi, e_lo, jnp.zeros((LANES - 3 * HEADS, rows), F32)], axis=0
    )
    et[...] = jnp.transpose(e_pad).astype(BF16)
    stats = jnp.where(lane < HEADS, peak, mm(ot[...], et[...]))
    for c in range(2):
        part_own[c, :, width : width + LANES] = stats[c * mine : (c + 1) * mine]
    loads[4].wait()

    def pool(j, carry):
        cols = pl.ds(pl.multiple_of(j * CHUNK, CHUNK), CHUNK)
        value = mm(p[...], wv[:, cols])
        v[:, cols] = value
        x_hi, x_lo = pieces(mm(et[...], hm[:, cols]) * value, 2)
        total = mm(ot[...], x_hi.astype(BF16)) + mm(ot[...], x_lo.astype(BF16))
        for c in range(2):
            part_own[c, :, cols] = total[c * mine : (c + 1) * mine]
        return carry

    lax.fori_loop(0, chunks, pool, 0)
    loads[5].wait()
    t_img[(core * nx + x) * nz + z] = text[...]

    pl.semaphore_wait(barrier, len(greeted))
    to_sibling(part_own.at[1 - core], part_in, 0)
    t_here = (core * nx + x) * nz
    slabs = lambda ref, n: ref.at[pl.ds(0, n)]
    spread(z_peers, lambda k: text, t_img.at[t_here + z], 1, slabs(t_img, nz - 1))

    arrived(part_in, 0)
    lane_m = lax.broadcasted_iota(jnp.int32, (mine, LANES), 1)
    stat_a = part_own[core, :, width : width + LANES]
    stat_b = part_in[:, width : width + LANES]
    top = jnp.maximum(stat_a, stat_b)
    chip_stats = jnp.where(lane_m < HEADS, top, 0.0)
    scale = []
    for stat in (stat_a, stat_b):
        f = jnp.where(lane_m < HEADS, jnp.exp(stat - top), 0.0)
        chip_stats += stat * (pltpu.roll(f, HEADS, 1) + pltpu.roll(f, 2 * HEADS, 1))
        f_hi, f_lo = pieces(f, 2)
        scale.append((f_hi + pltpu.roll(f_lo, HEADS, 1)).astype(BF16))
    for k in range(nq):
        acc_out[k, :, width : width + LANES] = chip_stats[k * IMG : (k + 1) * IMG]
    for j in range(chunks):
        cols = slice(j * CHUNK, (j + 1) * CHUNK)
        total = (
            mm(scale[0], hm[:, cols]) * part_own[core, :, cols]
            + mm(scale[1], hm[:, cols]) * part_in[:, cols]
        )
        for k in range(nq):
            acc_out[k, :, cols] = total[k * IMG : (k + 1) * IMG]
    spread(far_peers + near_peers, lambda k: acc_out.at[k], acc_in.at[q], 2, slabs(acc_in, nq - 1))
    acc_in[q] = acc_out[q]

    arrived(slabs(t_img, nz - 1), 1)
    x_part = t_img.at[pl.ds(t_here, nz)]
    spread(x_peers, lambda k: x_part, x_part, 3, slabs(t_img, (nx - 1) * nz))
    arrived(slabs(t_img, (nx - 1) * nz), 3)
    t_half = lambda c: t_img.at[pl.ds(c * nx * nz, nx * nz)]
    to_sibling(t_half(core), t_half(core), 4)
    loads[6].wait()

    arrived(slabs(acc_in, nq - 1), 2)
    lane4 = lax.broadcasted_iota(jnp.int32, (IMG, LANES), 1)
    heads4 = lane4 < HEADS
    parts = [acc_in[k, :, width : width + LANES] for k in range(nq)]
    m = parts[0]
    for part in parts[1:]:
        m = jnp.maximum(m, part)
    factors = []
    denom = jnp.zeros((IMG, LANES), F32)
    for part in parts:
        f = jnp.exp(part - m)
        mass = pltpu.roll(part, LANES - HEADS, 1) + pltpu.roll(part, LANES - 2 * HEADS, 1)
        factors.append(f)
        denom = denom + f * mass
    denom = jnp.where(heads4, denom, 1.0)
    lse = m + jnp.log(denom)
    for k, f in enumerate(factors):
        f_hi, f_lo = pieces(jnp.where(heads4, f / denom, 0.0), 2)
        fs[k * IMG : (k + 1) * IMG, :] = f_hi + pltpu.roll(f_lo, HEADS, 1)
    factor = mm(fs[...].astype(BF16), hm[...])
    pooled = jnp.zeros((IMG, width), F32)
    for k in range(nq):
        pooled = pooled + factor[k * IMG : (k + 1) * IMG] * acc_in[k, :, 0:width]
    pooled_buf[...] = pooled
    embeds = three(mm(small_rows(pooled, rows16), wo[...]))
    norm = jnp.sqrt(jnp.sum(embeds * embeds, axis=1, keepdims=True) + EPS)
    unit = embeds / norm
    unit_plane[xy] = unit
    u_here = unit_plane.at[xy]
    spread(y_peers, lambda k: u_here, u_here, 5, slabs(unit_plane, ny - 1))

    arrived(t_half(1 - core), 4)
    ntext = 2 * nx * nz * IMG
    for k in range(2 * nx * nz):
        tf[k * IMG : (k + 1) * IMG, :] = t_img[k].astype(F32)
    texts = tf[...]
    tb = texts.astype(BF16)
    inv = 1.0 / jnp.sqrt(jnp.sum(texts * texts, axis=1, keepdims=True) + EPS)
    inv_row = jnp.transpose(jnp.broadcast_to(inv, (ntext, LANES)))[0:1, :]
    temper = jnp.exp(logit_scale[...].reshape(1, 1))
    offset = logit_bias[...].reshape(1, 1)

    def block_signal(u_pieces, tb_, inv_, image_slab, text_slab):
        n, t = u_pieces[0].shape[0], tb_.shape[0]
        dots = mm_nt(jnp.concatenate(u_pieces, axis=0).astype(BF16), tb_)
        dots = dots[0:n] + dots[n : 2 * n] + dots[2 * n : 3 * n]
        logits = temper * (dots * inv_) + offset
        row = lax.broadcasted_iota(jnp.int32, (n, t), 0)
        col = lax.broadcasted_iota(jnp.int32, (n, t), 1)
        positive = ((row >> 2) == image_slab) & (col - text_slab * IMG == (row & (IMG - 1)))
        return 1.0 / (1.0 + jnp.exp(-logits)) - jnp.where(positive, 1.0, 0.0)

    arrived(slabs(unit_plane, ny - 1), 5)
    nline = ny * IMG
    for k in range(ny):
        u16[k * IMG : (k + 1) * IMG, :] = unit_plane[k * nx + x]
    signal = block_signal(pieces(u16[...], 3), tb, inv_row, y, (core * nx + x) * nz + z)
    di = mm(stacked(signal * inv_row, 3), tb)
    di = di[0:nline] + di[nline : 2 * nline] + di[2 * nline : 3 * nline]
    for k in range(ny):
        di_out[k] = di[k * IMG : (k + 1) * IMG]
    spread(y_peers, lambda k: di_out.at[k], di_in.at[y], 6, slabs(di_in, ny - 1))
    spread(rest_peers, lambda k: u_here, u_here, 7, slabs(unit_plane, (nx - 1) * ny))
    di_in[y] = di_out[y]

    arrived(slabs(di_in, ny - 1), 6)
    dunit = di_in[0]
    for k in range(1, ny):
        dunit = dunit + di_in[k]
    dunit = dunit * (temper * LOSS_SCALE)
    unit = unit_plane[xy]
    embed_grad = (dunit - unit * jnp.sum(unit * dunit, axis=1, keepdims=True)) / norm
    pooled_grad = three(mm_nt(small_rows(embed_grad, rows16), wo[...]))
    mass = three(mm_nt(small_rows(pooled_grad * pooled_buf[...], rows16), hm[...]))
    pg_all[core, q, :, 0:width] = pooled_grad
    pg_all[core, q, :, width : width + LANES] = jnp.where(
        heads4, lse, jnp.where(lane4 < 2 * HEADS, mass, 0.0)
    )
    pg_here = pg_all.at[core, q]
    near = pg_all.at[core, pl.ds(xh * nz, nz)]
    spread(far_peers, lambda k: pg_here, pg_here, 9, pg_all.at[0, pl.ds(0, nq - nz)])
    spread(near_peers, lambda k: pg_here, pg_here, 10, pg_all.at[0, pl.ds(0, nz - 1)])

    arrived(slabs(unit_plane, (nx - 1) * ny), 7)
    for k in range(nxy):
        u64[k * IMG : (k + 1) * IMG, :] = unit_plane[k]
    for c in range(2):
        here = pl.ds(pl.multiple_of((c * nx + x) * nz * IMG, nz * IMG), nz * IMG)
        tt[c * nz * IMG : (c + 1) * nz * IMG, :] = tf[here, :]
    line_texts = tt[...]
    line_inv = 1.0 / jnp.sqrt(jnp.sum(line_texts * line_texts, axis=1, keepdims=True) + EPS)
    line_inv = jnp.transpose(jnp.broadcast_to(line_inv, (LANES, LANES)))[0:1, :]
    u_pieces = pieces(u64[...], 3)
    signal = block_signal(u_pieces, line_texts.astype(BF16), line_inv, xy, core * nz + z)
    s_hi, s_lo = pieces(signal, 2)
    gap = -3 * nxy * IMG % LANES
    s_pad = jnp.concatenate([s_hi, s_hi, s_lo, jnp.zeros((gap, LANES), F32)], axis=0)
    u_pad = jnp.concatenate(
        [u_pieces[0], u_pieces[1], u_pieces[0], jnp.zeros((gap, width), F32)], axis=0
    )
    td = mm(jnp.transpose(s_pad).astype(BF16), u_pad.astype(BF16))
    for c in range(2):
        for k in range(nz):
            r = (c * nz + k) * IMG
            td_out[c, k] = td[r : r + IMG]
    to_sibling(td_out.at[1 - core], td_mid, 8)

    arrived(pg_all.at[0, pl.ds(0, nz - 1)], 10)
    to_sibling(near, near, 11)
    arrived(td_mid, 8)
    for k in range(nz):
        td_out[core, k] = td_out[core, k] + td_mid[k]
    spread(z_peers, lambda k: td_out.at[core, k], td_in.at[z], 12, slabs(td_in, nz - 1))
    td_in[z] = td_out[core, z]
    arrived(pg_all.at[0, pl.ds(0, nq - nz)], 9)
    for k in range(X_HIGH - 1):
        part = pg_all.at[core, pl.ds(lax.rem(xh + 1 + k, X_HIGH) * nz, nz)]
        to_sibling(part, part, 13 + k)
    for k in range(nq):
        pgm[core, k * IMG : (k + 1) * IMG, :] = pg_all[core, k]
    arrived(near, 11)
    for k in range(X_HIGH - 1):
        arrived(near, 13 + k)

    def store(j):
        cols = slice(j * CHUNK, (j + 1) * CHUNK)
        return pltpu.make_async_copy(out.at[:, cols], g_patch.at[:, cols], load_sem.at[7 + j])

    for k in range(nq):
        pgm[1 - core, k * IMG : (k + 1) * IMG, :] = pg_all[1 - core, k]
    row_stats = jnp.concatenate([pgm[0, :, width:], pgm[1, :, width:]], axis=0)
    row_stats = mm(stacked(jnp.transpose(row_stats)[0 : 2 * HEADS], 3), ot[...])
    row_stats = (
        row_stats[0 : 2 * HEADS] + row_stats[2 * HEADS : 4 * HEADS] + row_stats[4 * HEADS : 6 * HEADS]
    )
    own_o = jnp.transpose(jnp.concatenate([ot_f, ot_f], axis=0)).astype(BF16)
    pg = jnp.concatenate([pgm[0, :, 0:width], pgm[1, :, 0:width]], axis=0)
    pgr = mm(own_o, stacked(pg, 2))
    d_hi, d_lo = pieces(pgr * v[...], 2)
    dw = mm_nt(hm[0:HEADS, :], d_hi.astype(BF16)) + mm_nt(hm[0:HEADS, :], d_lo.astype(BF16))
    w = jnp.exp(st[...] - row_stats[0:HEADS])
    ds = w * (dw - row_stats[HEADS : 2 * HEADS])
    w_hi, w_lo = pieces(w, 2)
    ds_hi, ds_lo = pieces(ds, 2)
    wt = jnp.transpose(
        jnp.concatenate([w_hi, w_lo, blank, ds_hi, ds_hi, ds_lo, blank, blank], axis=0)
    ).astype(BF16)
    vg[...] = stacked(mm(wt, hm[...]) * pgr, 2)
    et[...] = wt

    for j in range(chunks):
        cols = slice(j * CHUNK, (j + 1) * CHUNK)
        g = mm_nt(vg[...], wv[cols, :])
        g = g[0:rows] + g[rows : 2 * rows] + mm(et[...], kpr[:, cols])
        out[:, cols] = g.astype(BF16)
        store(j).start()

    arrived(slabs(td_in, nz - 1), 12)
    text_dunit = td_in[0]
    for k in range(1, nz):
        text_dunit = text_dunit + td_in[k]
    text_dunit = text_dunit * (temper * LOSS_SCALE)
    own_text = text[...].astype(F32)
    text_norm = jnp.sqrt(jnp.sum(own_text * own_text, axis=1, keepdims=True) + EPS)
    text_unit = own_text / text_norm
    g_text[...] = (
        (text_dunit - text_unit * jnp.sum(text_unit * text_dunit, axis=1, keepdims=True))
        / text_norm
    ).astype(BF16)

    for whole, n in pending:
        remote(whole, whole, n, sibling).wait_send()
    for j in range(chunks):
        store(j).wait()


def hand_over(patch_in, text_in, patch_out, text_out, patch, text, sem):
    rows = patch.shape[0] // 2
    halves = [slice(0, rows), slice(rows, 2 * rows)]
    here = [
        (patch_in.at[halves[0]], patch.at[halves[0]], patch_out.at[halves[0]]),
        (patch_in.at[halves[1]], patch.at[halves[1]], patch_out.at[halves[1]]),
        (text_in, text, text_out),
    ]
    first = [pltpu.make_async_copy(a, b, sem.at[k]) for k, (a, b, _) in enumerate(here)]
    then = [pltpu.make_async_copy(b, c, sem.at[3 + k]) for k, (_, b, c) in enumerate(here)]
    for copy in first:
        copy.start()
    for arrived, copy in zip(first, then):
        arrived.wait()
        copy.start()
    for copy in then:
        copy.wait()


def local(nb, ng, patches, owner, slot, text, probe, w_key, w_value, w_out, scale, bias):
    rows, width = patches.shape
    nq = ng // 2
    nz = nq // X_HIGH
    nx = X_LOW * X_HIGH
    ny = nb // X_LOW
    nxy = nx * ny
    mine = nq * IMG
    wide = width + LANES
    vmem = pl.BlockSpec(memory_space=pltpu.VMEM)
    anywhere = pl.BlockSpec(memory_space=pl.ANY)
    weight = pltpu.VMEM((width, width), BF16)
    dma = pltpu.SemaphoreType.DMA
    shapes = (
        jax.ShapeDtypeStruct((rows, width), BF16),
        jax.ShapeDtypeStruct((IMG, width), BF16),
    )
    grads = pl.pallas_call(
        functools.partial(kernel, nb, ng),
        out_shape=shapes,
        in_specs=[anywhere] * 4 + [vmem] + [anywhere] * 3 + [vmem, vmem],
        out_specs=(anywhere, vmem),
        scratch_shapes=[
            pltpu.VMEM(owner.shape, jnp.int32),
            pltpu.VMEM(slot.shape, jnp.int32),
            pltpu.VMEM(text.shape, BF16),
            weight,
            weight,
            weight,
            pltpu.VMEM((rows, width), BF16),
            pltpu.VMEM((rows, width), F32),
            pltpu.VMEM((HEADS, rows), F32),
            pltpu.VMEM((LANES, width), BF16),
            pltpu.VMEM((3 * HEADS, width), BF16),
            pltpu.VMEM((LANES, width), BF16),
            pltpu.VMEM((2 * mine, rows), BF16),
            pltpu.VMEM((rows, LANES), BF16),
            pltpu.VMEM((2, mine, wide), F32),
            pltpu.VMEM((mine, wide), F32),
            pltpu.VMEM((nq, IMG, wide), F32),
            pltpu.VMEM((nq, IMG, wide), F32),
            pltpu.VMEM((mine, LANES), F32),
            pltpu.VMEM((16, width), F32),
            pltpu.VMEM((IMG, width), F32),
            pltpu.VMEM((nxy, IMG, width), F32),
            pltpu.VMEM((ny * IMG, width), F32),
            pltpu.VMEM((ny, IMG, width), F32),
            pltpu.VMEM((ny, IMG, width), F32),
            pltpu.VMEM((nxy * IMG, width), F32),
            pltpu.VMEM((2 * nx * nz, IMG, width), BF16),
            pltpu.VMEM((2 * nx * nz * IMG, width), F32),
            pltpu.VMEM((LANES, width), F32),
            pltpu.VMEM((2, nz, IMG, width), F32),
            pltpu.VMEM((nz, IMG, width), F32),
            pltpu.VMEM((nz, IMG, width), F32),
            pltpu.VMEM((2, nq, IMG, wide), F32),
            pltpu.VMEM((2, mine, wide), F32),
            pltpu.VMEM((2 * rows, width), BF16),
            pltpu.VMEM((rows, width), BF16),
            dma((10,)),
            dma((16,)),
            dma((16,)),
        ],
        compiler_params=pltpu.CompilerParams(
            collective_id=0, has_side_effects=True, vmem_limit_bytes=56 * 2**20
        ),
        name="pool_contrast",
    )(patches, owner, slot, text, probe, w_key, w_value, w_out, scale, bias)
    return pl.pallas_call(
        hand_over,
        out_shape=shapes,
        in_specs=[anywhere, anywhere],
        out_specs=(anywhere, anywhere),
        scratch_shapes=[
            pltpu.VMEM((rows, width), BF16),
            pltpu.VMEM(text.shape, BF16),
            dma((6,)),
        ],
        compiler_params=pltpu.CompilerParams(vmem_limit_bytes=56 * 2**20),
        name="hand_over",
    )(*grads)


def solution(mesh):
    nb = mesh.shape["blk"]
    ng = mesh.shape["group"]
    return jax.shard_map(
        functools.partial(local, nb, ng),
        mesh=mesh,
        in_specs=(
            P(("blk", "group"), None),
            P("blk", None, None),
            P("blk", None, None),
            P(("blk", "group"), None),
            P(),
            P(),
            P(),
            P(),
            P(),
            P(),
        ),
        out_specs=(P(("blk", "group"), None), P(("blk", "group"), None)),
        check_vma=False,
    )
```

```python
import functools
import math

import jax
import jax.numpy as jnp
from jax import lax
from jax.experimental import pallas as pl
from jax.experimental.pallas import tpu as pltpu
from jax.sharding import PartitionSpec as P

HEADS = 16
IMG = 4
X_LOW, X_HIGH = 2, 2
LANES = 128
CHUNK = 384
SPLIT = 512
LOSS_SCALE = 256.0
EPS = 1e-06
LOW = -1e30

F32 = jnp.float32
BF16 = jnp.bfloat16
MESH = pl.DeviceIdType.MESH


def mm(a, b):
    return lax.dot_general(a, b, (((1,), (0,)), ((), ())), preferred_element_type=F32)


def mm_nt(a, b):
    return lax.dot_general(a, b, (((1,), (1,)), ((), ())), preferred_element_type=F32)


def pieces(x, count):
    out = []
    for _ in range(count - 1):
        top = x.astype(BF16).astype(F32)
        out.append(top)
        x = x - top
    out.append(x.astype(BF16).astype(F32))
    return out


def stacked(x, count):
    return jnp.concatenate(pieces(x, count), axis=0).astype(BF16)


def small_rows(x, buf):
    for k, piece in enumerate(pieces(x, 3)):
        buf[k * IMG : (k + 1) * IMG, :] = piece
    return buf[...].astype(BF16)


def three(y):
    return y[0:IMG] + y[IMG : 2 * IMG] + y[2 * IMG : 3 * IMG]


def far(n):
    return [(n // 2 + ((j + 1) // 2) * (2 * ((j + 1) % 2) - 1)) % n for j in range(n)]


def kernel(
    nb,
    ng,
    patches,
    owner_in,
    slot_in,
    text_in,
    probe_in,
    w_key,
    w_value,
    w_out,
    logit_scale,
    logit_bias,
    g_patch,
    g_text,
    owner,
    slot,
    text,
    probe,
    wk,
    wv,
    wo,
    p,
    v,
    st,
    hm,
    kp3,
    kpr,
    ot,
    et,
    ob,
    part_own,
    part_in,
    acc_out,
    acc_in,
    fs,
    rows16,
    pooled_buf,
    unit_plane,
    u16,
    di_out,
    di_in,
    u64,
    t_img,
    tf,
    tt,
    td_out,
    td_mid,
    td_in,
    pg_all,
    pgm,
    vg,
    out,
    load_sem,
    send_sem,
    recv_sem,
):
    nq = ng // 2
    nz = nq // X_HIGH
    nx = X_LOW * X_HIGH
    ny = nb // X_LOW
    nxy = nx * ny
    mine = nq * IMG
    rows, width = patches.shape
    chunks = width // CHUNK
    head_width = width // HEADS
    blk = lax.axis_index("blk")
    grp = lax.axis_index("group")
    core = lax.rem(grp, 2)
    q = lax.div(grp, 2)
    z = lax.rem(q, nz)
    xh = lax.div(q, nz)
    y = lax.div(blk, X_LOW)
    x = xh * X_LOW + lax.rem(blk, X_LOW)
    xy = y * nx + x
    pending = []

    def at(x_, y_, z_, c_):
        x_high = lax.div(x_, X_LOW)
        return (y_ * X_LOW + x_ - x_high * X_LOW, (x_high * nz + z_) * 2 + c_)

    def ring(pos, n):
        return [pos if d == 0 else lax.rem(pos + d, n) for d in far(n)]

    sibling = at(x, y, z, 1 - core)
    ring_x, ring_y, ring_z = ring(x, nx), ring(y, ny), ring(z, nz)
    z_peers = [(k, at(x, y, k, core)) for k in ring_z[:-1]]
    x_peers = [(k, at(k, y, z, core)) for k in ring_x[:-1]]
    y_peers = [(k, at(x, k, z, core)) for k in ring_y[:-1]]
    rest_peers = [(j * nx + k, at(k, j, z, core)) for k in ring_x[:-1] for j in ring_y]
    far_peers = [
        (h * nz + k, (blk, (h * nz + k) * 2 + core)) for h in ring(xh, X_HIGH)[:-1] for k in ring_z
    ]
    near_peers = [(xh * nz + k, device) for k, device in z_peers]

    def remote(src, dst, n, device):
        return pltpu.make_async_remote_copy(
            src_ref=src,
            dst_ref=dst,
            send_sem=send_sem.at[n],
            recv_sem=recv_sem.at[n],
            device_id=device,
            device_id_type=MESH,
        )

    def spread(peers, src_of, dst, n, whole):
        for k, device in peers:
            remote(src_of(k), dst, n, device).start()
        pending.append((whole, n))

    def arrived(whole, n):
        remote(whole, whole, n, sibling).wait_recv()

    def to_sibling(src, dst, n):
        spread([(0, sibling)], lambda k: src, dst, n, src)

    pieces_of = [slice(j * CHUNK, (j + 1) * CHUNK) for j in range(chunks)]
    halves = [slice(0, SPLIT), slice(SPLIT, width)]

    def load(n, src, dst):
        copy = pltpu.make_async_copy(src, dst, load_sem.at[n])
        copy.start()
        return copy

    load_probe = load(chunks, probe_in, probe)
    load_rows = [
        load(chunks + 1, owner_in, owner),
        load(chunks + 2, slot_in, slot),
    ]
    load_k = [load(j, w_key.at[cols], wk.at[cols]) for j, cols in enumerate(pieces_of)]
    load_rows.append(load(chunks + 3, patches, p))
    load_text = [
        load(chunks + 4, text_in, text),
    ]
    late = chunks + 7
    load_v = [load(late + j, w_value.at[cols], wv.at[cols]) for j, cols in enumerate(pieces_of)]
    load_o = load(late + chunks, w_out, wo)

    barrier = pltpu.get_barrier_semaphore()

    greeted = far_peers + near_peers + rest_peers + y_peers + [(0, sibling)]
    for _, device in greeted:
        pl.semaphore_signal(barrier, inc=1, device_id=device, device_id_type=MESH)

    row_i = lax.broadcasted_iota(jnp.int32, (LANES, width), 0)
    col_i = lax.broadcasted_iota(jnp.int32, (LANES, width), 1)
    first = (row_i & (HEADS - 1)) * head_width
    in_head = (col_i >= first) & (col_i < first + head_width)
    hm[...] = jnp.where(in_head & (row_i < 3 * HEADS), 1.0, 0.0).astype(BF16)
    load_probe.wait()
    q3 = pieces(probe[...].reshape(1, width) / math.sqrt(head_width), 3)
    band = lax.broadcasted_iota(jnp.int32, (3 * HEADS, width), 0) // HEADS
    q_rows = jnp.where(band == 0, q3[0], jnp.where(band == 1, q3[1], q3[2]))
    table = (q_rows * hm[0 : 3 * HEADS, :].astype(F32)).astype(BF16)
    kpr[...] = jnp.zeros_like(kpr)
    for j, cols in enumerate(pieces_of):
        load_k[j].wait()
        kpt = mm_nt(table, wk[cols, :])
        kp = kpt[0:HEADS] + kpt[HEADS : 2 * HEADS] + kpt[2 * HEADS : 3 * HEADS]
        kp_pieces = pieces(kp, 3)
        kp3[:, cols] = jnp.concatenate(kp_pieces, axis=0).astype(BF16)
        kpr[3 * HEADS : 6 * HEADS, cols] = jnp.concatenate(
            [kp_pieces[0], kp_pieces[1], kp_pieces[0]], axis=0
        ).astype(BF16)
    rows16[...] = jnp.zeros_like(rows16)
    tt[...] = jnp.zeros_like(tt)

    load_rows[0].wait()
    load_rows[1].wait()
    own_owner = owner[0, pl.ds(grp, 1), :]
    code = (own_owner & 1) * mine + (own_owner >> 1) * IMG + slot[0, pl.ds(grp, 1), :]
    member = code == lax.broadcasted_iota(jnp.int32, (2 * mine, rows), 0)
    ot_f = jnp.where(member, 1.0, 0.0)
    ot[...] = ot_f.astype(BF16)

    load_rows[2].wait()
    s = mm_nt(kp3[...], p[...])
    scores = s[0:HEADS] + s[HEADS : 2 * HEADS] + s[2 * HEADS : 3 * HEADS]
    st[...] = scores
    lane = lax.broadcasted_iota(jnp.int32, (2 * mine, LANES), 1)
    peak = jnp.zeros((2 * mine, LANES), F32)
    for h in range(HEADS):
        top = jnp.max(jnp.where(member, scores[h : h + 1, :], LOW), axis=1, keepdims=True)
        peak = jnp.where(lane == h, top, peak)
    peak_t = jnp.transpose(peak)[0:HEADS]
    shift = mm(stacked(peak_t, 3), ot[...])
    shift = shift[0:HEADS] + shift[HEADS : 2 * HEADS] + shift[2 * HEADS : 3 * HEADS]
    e_hi, e_lo = pieces(jnp.exp(scores - shift), 2)
    blank = jnp.zeros((HEADS, rows), F32)
    e_pad = jnp.concatenate(
        [blank, e_hi, e_lo, jnp.zeros((LANES - 3 * HEADS, rows), F32)], axis=0
    )
    et[...] = jnp.transpose(e_pad).astype(BF16)
    stats = jnp.where(lane < HEADS, peak, mm(ot[...], et[...]))
    for c in range(2):
        part_own[c, :, width : width + LANES] = stats[c * mine : (c + 1) * mine]
    for copy in load_v:
        copy.wait()
    for cols in halves:
        value = mm(p[...], wv[:, cols])
        v[:, cols] = value
        x_hi, x_lo = pieces(mm(et[...], hm[:, cols]) * value, 2)
        total = mm(ot[...], x_hi.astype(BF16)) + mm(ot[...], x_lo.astype(BF16))
        for c in range(2):
            part_own[c, :, cols] = total[c * mine : (c + 1) * mine]
    for copy in load_text:
        copy.wait()
    t_img[(core * nx + x) * nz + z] = text[...]

    pl.semaphore_wait(barrier, len(greeted))
    part_cols = [slice(width, width + LANES)] + halves
    for j, cols in enumerate(part_cols):
        to_sibling(part_own.at[1 - core, :, cols], part_in.at[:, cols], 16 + j)
    t_here = (core * nx + x) * nz
    slabs = lambda ref, n: ref.at[pl.ds(0, n)]
    spread(z_peers, lambda k: text, t_img.at[t_here + z], 1, slabs(t_img, nz - 1))

    arrived(part_in.at[:, part_cols[0]], 16)
    lane_m = lax.broadcasted_iota(jnp.int32, (mine, LANES), 1)
    stat_a = part_own[core, :, width : width + LANES]
    stat_b = part_in[:, width : width + LANES]
    top = jnp.maximum(stat_a, stat_b)
    chip_stats = jnp.where(lane_m < HEADS, top, 0.0)
    scale = []
    for stat in (stat_a, stat_b):
        f = jnp.where(lane_m < HEADS, jnp.exp(stat - top), 0.0)
        chip_stats += stat * (pltpu.roll(f, HEADS, 1) + pltpu.roll(f, 2 * HEADS, 1))
        f_hi, f_lo = pieces(f, 2)
        scale.append((f_hi + pltpu.roll(f_lo, HEADS, 1)).astype(BF16))
    for k in range(nq):
        acc_out[k, :, width : width + LANES] = chip_stats[k * IMG : (k + 1) * IMG]
    for j, cols in enumerate(halves):
        arrived(part_in.at[:, cols], 17 + j)
        total = (
            mm(scale[0], hm[:, cols]) * part_own[core, :, cols]
            + mm(scale[1], hm[:, cols]) * part_in[:, cols]
        )
        for k in range(nq):
            acc_out[k, :, cols] = total[k * IMG : (k + 1) * IMG]
    spread(far_peers + near_peers, lambda k: acc_out.at[k], acc_in.at[q], 2, slabs(acc_in, nq - 1))
    acc_in[q] = acc_out[q]

    arrived(slabs(t_img, nz - 1), 1)
    x_part = t_img.at[pl.ds(t_here, nz)]
    spread(x_peers, lambda k: x_part, x_part, 3, slabs(t_img, (nx - 1) * nz))
    arrived(slabs(t_img, (nx - 1) * nz), 3)
    t_half = lambda c: t_img.at[pl.ds(c * nx * nz, nx * nz)]
    to_sibling(t_half(core), t_half(core), 4)
    load_o.wait()

    for c in range(2):
        half = ot_f[c * mine : (c + 1) * mine]
        ob[c] = jnp.transpose(jnp.concatenate([half, half], axis=0)).astype(BF16)

    arrived(slabs(acc_in, nq - 1), 2)
    lane4 = lax.broadcasted_iota(jnp.int32, (IMG, LANES), 1)
    heads4 = lane4 < HEADS
    parts = [acc_in[k, :, width : width + LANES] for k in range(nq)]
    m = parts[0]
    for part in parts[1:]:
        m = jnp.maximum(m, part)
    factors = []
    denom = jnp.zeros((IMG, LANES), F32)
    for part in parts:
        f = jnp.exp(part - m)
        mass = pltpu.roll(part, LANES - HEADS, 1) + pltpu.roll(part, LANES - 2 * HEADS, 1)
        factors.append(f)
        denom = denom + f * mass
    denom = jnp.where(heads4, denom, 1.0)
    lse = m + jnp.log(denom)
    for k, f in enumerate(factors):
        f_hi, f_lo = pieces(jnp.where(heads4, f / denom, 0.0), 2)
        fs[k * IMG : (k + 1) * IMG, :] = f_hi + pltpu.roll(f_lo, HEADS, 1)
    factor = mm(fs[...].astype(BF16), hm[...])
    pooled = jnp.zeros((IMG, width), F32)
    for k in range(nq):
        pooled = pooled + factor[k * IMG : (k + 1) * IMG] * acc_in[k, :, 0:width]
    pooled_buf[...] = pooled
    embeds = three(mm(small_rows(pooled, rows16), wo[...]))
    norm = jnp.sqrt(jnp.sum(embeds * embeds, axis=1, keepdims=True) + EPS)
    unit = embeds / norm
    unit_plane[xy] = unit
    u_here = unit_plane.at[xy]
    spread(y_peers, lambda k: u_here, u_here, 5, slabs(unit_plane, ny - 1))

    arrived(t_half(1 - core), 4)
    ntext = 2 * nx * nz * IMG
    for k in range(2 * nx * nz):
        tf[k * IMG : (k + 1) * IMG, :] = t_img[k].astype(F32)
    texts = tf[...]
    tb = texts.astype(BF16)
    inv = 1.0 / jnp.sqrt(jnp.sum(texts * texts, axis=1, keepdims=True) + EPS)
    inv_row = jnp.transpose(jnp.broadcast_to(inv, (ntext, LANES)))[0:1, :]
    temper = jnp.exp(jnp.full((1, 1), logit_scale[0], F32))
    offset = logit_bias[0]

    def block_signal(u_pieces, tb_, inv_, image_slab, text_slab):
        n, t = u_pieces[0].shape[0], tb_.shape[0]
        dots = mm_nt(jnp.concatenate(u_pieces, axis=0).astype(BF16), tb_)
        dots = dots[0:n] + dots[n : 2 * n] + dots[2 * n : 3 * n]
        logits = temper * (dots * inv_) + offset
        row = lax.broadcasted_iota(jnp.int32, (n, t), 0)
        col = lax.broadcasted_iota(jnp.int32, (n, t), 1)
        positive = ((row >> 2) == image_slab) & (col - text_slab * IMG == (row & (IMG - 1)))
        return 1.0 / (1.0 + jnp.exp(-logits)) - jnp.where(positive, 1.0, 0.0)

    arrived(slabs(unit_plane, ny - 1), 5)
    nline = ny * IMG
    for k in range(ny):
        u16[k * IMG : (k + 1) * IMG, :] = unit_plane[k * nx + x]
    signal = block_signal(pieces(u16[...], 3), tb, inv_row, y, (core * nx + x) * nz + z)
    di = mm(stacked(signal * inv_row, 3), tb)
    di = di[0:nline] + di[nline : 2 * nline] + di[2 * nline : 3 * nline]
    for k in range(ny):
        di_out[k] = di[k * IMG : (k + 1) * IMG]
    spread(y_peers, lambda k: di_out.at[k], di_in.at[y], 6, slabs(di_in, ny - 1))
    spread(rest_peers, lambda k: u_here, u_here, 7, slabs(unit_plane, (nx - 1) * ny))
    di_in[y] = di_out[y]

    arrived(slabs(di_in, ny - 1), 6)
    dunit = di_in[0]
    for k in range(1, ny):
        dunit = dunit + di_in[k]
    dunit = dunit * (temper * LOSS_SCALE)
    unit = unit_plane[xy]
    embed_grad = (dunit - unit * jnp.sum(unit * dunit, axis=1, keepdims=True)) / norm
    pooled_grad = three(mm_nt(small_rows(embed_grad, rows16), wo[...]))
    mass = three(mm_nt(small_rows(pooled_grad * pooled_buf[...], rows16), hm[...]))
    pg_all[core, q, :, 0:width] = pooled_grad
    pg_all[core, q, :, width : width + LANES] = jnp.where(
        heads4, lse, jnp.where(lane4 < 2 * HEADS, mass, 0.0)
    )
    pg_here = pg_all.at[core, q]
    near = pg_all.at[core, pl.ds(xh * nz, nz)]
    spread(far_peers, lambda k: pg_here, pg_here, 9, pg_all.at[0, pl.ds(0, nq - nz)])
    spread(near_peers, lambda k: pg_here, pg_here, 10, pg_all.at[0, pl.ds(0, nz - 1)])

    arrived(slabs(unit_plane, (nx - 1) * ny), 7)
    for k in range(nxy):
        u64[k * IMG : (k + 1) * IMG, :] = unit_plane[k]
    for c in range(2):
        here = pl.ds(pl.multiple_of((c * nx + x) * nz * IMG, nz * IMG), nz * IMG)
        tt[c * nz * IMG : (c + 1) * nz * IMG, :] = tf[here, :]
    line_texts = tt[...]
    line_inv = 1.0 / jnp.sqrt(jnp.sum(line_texts * line_texts, axis=1, keepdims=True) + EPS)
    line_inv = jnp.transpose(jnp.broadcast_to(line_inv, (LANES, LANES)))[0:1, :]
    u_pieces = pieces(u64[...], 3)
    signal = block_signal(u_pieces, line_texts.astype(BF16), line_inv, xy, core * nz + z)
    s_hi, s_lo = pieces(signal, 2)
    gap = -3 * nxy * IMG % LANES
    s_pad = jnp.concatenate([s_hi, s_hi, s_lo, jnp.zeros((gap, LANES), F32)], axis=0)
    u_pad = jnp.concatenate(
        [u_pieces[0], u_pieces[1], u_pieces[0], jnp.zeros((gap, width), F32)], axis=0
    )
    td = mm(jnp.transpose(s_pad).astype(BF16), u_pad.astype(BF16))
    for c in range(2):
        for k in range(nz):
            r = (c * nz + k) * IMG
            td_out[c, k] = td[r : r + IMG]
    to_sibling(td_out.at[1 - core], td_mid, 8)

    arrived(pg_all.at[0, pl.ds(0, nz - 1)], 10)
    to_sibling(near, near, 11)
    arrived(td_mid, 8)
    for k in range(nz):
        td_out[core, k] = td_out[core, k] + td_mid[k]
    spread(z_peers, lambda k: td_out.at[core, k], td_in.at[z], 12, slabs(td_in, nz - 1))
    td_in[z] = td_out[core, z]
    arrived(pg_all.at[0, pl.ds(0, nq - nz)], 9)
    for k in range(X_HIGH - 1):
        part = pg_all.at[core, pl.ds(lax.rem(xh + 1 + k, X_HIGH) * nz, nz)]
        to_sibling(part, part, 13 + k)
    for k in range(nq):
        pgm[core, k * IMG : (k + 1) * IMG, :] = pg_all[core, k]
    pgr = mm(ob[core], stacked(pgm[core, :, 0:width], 2))
    arrived(near, 11)
    for k in range(X_HIGH - 1):
        arrived(near, 13 + k)

    def store(j):
        cols = halves[j]
        return pltpu.make_async_copy(out.at[:, cols], g_patch.at[:, cols], load_sem.at[j])

    for k in range(nq):
        pgm[1 - core, k * IMG : (k + 1) * IMG, :] = pg_all[1 - core, k]
    row_stats = jnp.concatenate([pgm[0, :, width:], pgm[1, :, width:]], axis=0)
    row_stats = mm(stacked(jnp.transpose(row_stats)[0 : 2 * HEADS], 3), ot[...])
    row_stats = (
        row_stats[0 : 2 * HEADS] + row_stats[2 * HEADS : 4 * HEADS] + row_stats[4 * HEADS : 6 * HEADS]
    )
    pgr = pgr + mm(ob[1 - core], stacked(pgm[1 - core, :, 0:width], 2))
    w = jnp.exp(st[...] - row_stats[0:HEADS])
    gap = jnp.zeros((LANES - 2 * HEADS, rows), F32)
    w_t = jnp.transpose(jnp.concatenate(pieces(w, 2) + [gap], axis=0)).astype(BF16)
    vg[...] = stacked(mm(w_t, hm[...]) * pgr, 2)
    d_hi, d_lo = pieces(pgr * v[...], 2)
    dw = mm_nt(hm[0:HEADS, :], d_hi.astype(BF16)) + mm_nt(hm[0:HEADS, :], d_lo.astype(BF16))
    ds_hi, ds_lo = pieces(w * (dw - row_stats[HEADS : 2 * HEADS]), 2)
    ds_t = jnp.transpose(
        jnp.concatenate([blank, blank, blank, ds_hi, ds_hi, ds_lo, blank, blank], axis=0)
    ).astype(BF16)

    for j, cols in enumerate(halves):
        g = mm_nt(vg[...], wv[cols, :])
        g = g[0:rows] + g[rows : 2 * rows] + mm(ds_t, kpr[:, cols])
        out[:, cols] = g.astype(BF16)
        store(j).start()

    arrived(slabs(td_in, nz - 1), 12)
    text_dunit = td_in[0]
    for k in range(1, nz):
        text_dunit = text_dunit + td_in[k]
    text_dunit = text_dunit * (temper * LOSS_SCALE)
    own_text = text[...].astype(F32)
    text_norm = jnp.sqrt(jnp.sum(own_text * own_text, axis=1, keepdims=True) + EPS)
    text_unit = own_text / text_norm
    g_text[...] = (
        (text_dunit - text_unit * jnp.sum(text_unit * text_dunit, axis=1, keepdims=True))
        / text_norm
    ).astype(BF16)

    for whole, n in pending:
        remote(whole, whole, n, sibling).wait_send()
    for j in range(len(halves)):
        store(j).wait()


def hand_over(patch_in, text_in, patch_out, text_out, patch, text, sem):
    rows = patch.shape[0] // 2
    halves = [slice(0, rows), slice(rows, 2 * rows)]
    here = [
        (patch_in.at[halves[0]], patch.at[halves[0]], patch_out.at[halves[0]]),
        (patch_in.at[halves[1]], patch.at[halves[1]], patch_out.at[halves[1]]),
        (text_in, text, text_out),
    ]
    first = [pltpu.make_async_copy(a, b, sem.at[k]) for k, (a, b, _) in enumerate(here)]
    then = [pltpu.make_async_copy(b, c, sem.at[3 + k]) for k, (_, b, c) in enumerate(here)]
    for copy in first:
        copy.start()
    for arrived, copy in zip(first, then):
        arrived.wait()
        copy.start()
    for copy in then:
        copy.wait()


def local(nb, ng, patches, owner, slot, text, probe, w_key, w_value, w_out, scale, bias):
    rows, width = patches.shape
    nq = ng // 2
    nz = nq // X_HIGH
    nx = X_LOW * X_HIGH
    ny = nb // X_LOW
    nxy = nx * ny
    mine = nq * IMG
    wide = width + LANES
    vmem = pl.BlockSpec(memory_space=pltpu.VMEM)
    anywhere = pl.BlockSpec(memory_space=pl.ANY)
    weight = pltpu.VMEM((width, width), BF16)
    dma = pltpu.SemaphoreType.DMA
    shapes = (
        jax.ShapeDtypeStruct((rows, width), BF16),
        jax.ShapeDtypeStruct((IMG, width), BF16),
    )
    grads = pl.pallas_call(
        functools.partial(kernel, nb, ng),
        out_shape=shapes,
        in_specs=[anywhere] * 8 + [pl.BlockSpec(memory_space=pltpu.SMEM)] * 2,
        out_specs=(anywhere, vmem),
        scratch_shapes=[
            pltpu.VMEM(owner.shape, jnp.int32),
            pltpu.VMEM(slot.shape, jnp.int32),
            pltpu.VMEM(text.shape, BF16),
            pltpu.VMEM((width,), F32),
            weight,
            weight,
            weight,
            pltpu.VMEM((rows, width), BF16),
            pltpu.VMEM((rows, width), F32),
            pltpu.VMEM((HEADS, rows), F32),
            pltpu.VMEM((LANES, width), BF16),
            pltpu.VMEM((3 * HEADS, width), BF16),
            pltpu.VMEM((LANES, width), BF16),
            pltpu.VMEM((2 * mine, rows), BF16),
            pltpu.VMEM((rows, LANES), BF16),
            pltpu.VMEM((2, rows, 2 * mine), BF16),
            pltpu.VMEM((2, mine, wide), F32),
            pltpu.VMEM((mine, wide), F32),
            pltpu.VMEM((nq, IMG, wide), F32),
            pltpu.VMEM((nq, IMG, wide), F32),
            pltpu.VMEM((mine, LANES), F32),
            pltpu.VMEM((16, width), F32),
            pltpu.VMEM((IMG, width), F32),
            pltpu.VMEM((nxy, IMG, width), F32),
            pltpu.VMEM((ny * IMG, width), F32),
            pltpu.VMEM((ny, IMG, width), F32),
            pltpu.VMEM((ny, IMG, width), F32),
            pltpu.VMEM((nxy * IMG, width), F32),
            pltpu.VMEM((2 * nx * nz, IMG, width), BF16),
            pltpu.VMEM((2 * nx * nz * IMG, width), F32),
            pltpu.VMEM((LANES, width), F32),
            pltpu.VMEM((2, nz, IMG, width), F32),
            pltpu.VMEM((nz, IMG, width), F32),
            pltpu.VMEM((nz, IMG, width), F32),
            pltpu.VMEM((2, nq, IMG, wide), F32),
            pltpu.VMEM((2, mine, wide), F32),
            pltpu.VMEM((2 * rows, width), BF16),
            pltpu.VMEM((rows, width), BF16),
            dma((16,)),
            dma((20,)),
            dma((20,)),
        ],
        compiler_params=pltpu.CompilerParams(
            collective_id=0, has_side_effects=True, vmem_limit_bytes=56 * 2**20
        ),
        name="pool_contrast",
    )(patches, owner, slot, text, probe, w_key, w_value, w_out, scale, bias)
    return pl.pallas_call(
        hand_over,
        out_shape=shapes,
        in_specs=[anywhere, anywhere],
        out_specs=(anywhere, anywhere),
        scratch_shapes=[
            pltpu.VMEM((rows, width), BF16),
            pltpu.VMEM(text.shape, BF16),
            dma((6,)),
        ],
        compiler_params=pltpu.CompilerParams(vmem_limit_bytes=56 * 2**20),
        name="hand_over",
    )(*grads)


def solution(mesh):
    nb = mesh.shape["blk"]
    ng = mesh.shape["group"]
    return jax.shard_map(
        functools.partial(local, nb, ng),
        mesh=mesh,
        in_specs=(
            P(("blk", "group"), None),
            P("blk", None, None),
            P("blk", None, None),
            P(("blk", "group"), None),
            P(),
            P(),
            P(),
            P(),
            P(),
            P(),
        ),
        out_specs=(P(("blk", "group"), None), P(("blk", "group"), None)),
        check_vma=False,
    )
```

```python
import functools
import math

import jax
import jax.numpy as jnp
from jax import lax
from jax.experimental import pallas as pl
from jax.experimental.pallas import tpu as pltpu
from jax.sharding import PartitionSpec as P

HEADS = 16
IMG = 4
X_LOW, X_HIGH = 2, 2
LANES = 128
CHUNK = 384
SPLIT = 512
LOSS_SCALE = 256.0
EPS = 1e-06
LOW = -1e30

F32 = jnp.float32
BF16 = jnp.bfloat16
MESH = pl.DeviceIdType.MESH


def mm(a, b):
    return lax.dot_general(a, b, (((1,), (0,)), ((), ())), preferred_element_type=F32)


def mm_nt(a, b):
    return lax.dot_general(a, b, (((1,), (1,)), ((), ())), preferred_element_type=F32)


def pieces(x, count):
    out = []
    for _ in range(count - 1):
        top = x.astype(BF16).astype(F32)
        out.append(top)
        x = x - top
    out.append(x.astype(BF16).astype(F32))
    return out


def stacked(x, count):
    return jnp.concatenate(pieces(x, count), axis=0).astype(BF16)


def small_rows(x, buf):
    for k, piece in enumerate(pieces(x, 3)):
        buf[k * IMG : (k + 1) * IMG, :] = piece
    return buf[...].astype(BF16)


def three(y):
    return y[0:IMG] + y[IMG : 2 * IMG] + y[2 * IMG : 3 * IMG]


def far(n):
    return [(n // 2 + ((j + 1) // 2) * (2 * ((j + 1) % 2) - 1)) % n for j in range(n)]


def kernel(
    nb,
    ng,
    patches,
    owner_in,
    slot_in,
    text_in,
    probe_in,
    w_key,
    w_value,
    w_out,
    logit_scale,
    logit_bias,
    g_patch,
    g_text,
    owner,
    slot,
    text,
    probe,
    wk,
    wv,
    wo,
    p,
    v,
    st,
    hm,
    kp3,
    kpr,
    ot,
    et,
    ob,
    part_own,
    part_in,
    acc_out,
    acc_in,
    fs,
    rows16,
    pooled_buf,
    unit_plane,
    u16,
    di_out,
    di_in,
    u64,
    t_img,
    tf,
    tt,
    td_out,
    td_mid,
    td_in,
    pg_all,
    pgm,
    vg,
    out,
    text_out,
    load_sem,
    send_sem,
    recv_sem,
):
    nq = ng // 2
    nz = nq // X_HIGH
    nx = X_LOW * X_HIGH
    ny = nb // X_LOW
    nxy = nx * ny
    mine = nq * IMG
    rows, width = patches.shape
    chunks = width // CHUNK
    head_width = width // HEADS
    blk = lax.axis_index("blk")
    grp = lax.axis_index("group")
    core = lax.rem(grp, 2)
    q = lax.div(grp, 2)
    z = lax.rem(q, nz)
    xh = lax.div(q, nz)
    y = lax.div(blk, X_LOW)
    x = xh * X_LOW + lax.rem(blk, X_LOW)
    xy = y * nx + x
    pending = []

    def at(x_, y_, z_, c_):
        x_high = lax.div(x_, X_LOW)
        return (y_ * X_LOW + x_ - x_high * X_LOW, (x_high * nz + z_) * 2 + c_)

    def ring(pos, n):
        return [pos if d == 0 else lax.rem(pos + d, n) for d in far(n)]

    sibling = at(x, y, z, 1 - core)
    ring_x, ring_y, ring_z = ring(x, nx), ring(y, ny), ring(z, nz)
    z_peers = [(k, at(x, y, k, core)) for k in ring_z[:-1]]
    x_peers = [(k, at(k, y, z, core)) for k in ring_x[:-1]]
    y_peers = [(k, at(x, k, z, core)) for k in ring_y[:-1]]
    rest_peers = [(j * nx + k, at(k, j, z, core)) for k in ring_x[:-1] for j in ring_y]
    far_peers = [
        (h * nz + k, (blk, (h * nz + k) * 2 + core)) for h in ring(xh, X_HIGH)[:-1] for k in ring_z
    ]
    near_peers = [(xh * nz + k, device) for k, device in z_peers]

    def remote(src, dst, n, device):
        return pltpu.make_async_remote_copy(
            src_ref=src,
            dst_ref=dst,
            send_sem=send_sem.at[n],
            recv_sem=recv_sem.at[n],
            device_id=device,
            device_id_type=MESH,
        )

    def spread(peers, src_of, dst, n, whole):
        for k, device in peers:
            remote(src_of(k), dst, n, device).start()
        pending.append((whole, n))

    def arrived(whole, n):
        remote(whole, whole, n, sibling).wait_recv()

    def settle(sends):
        for whole, n in sends:
            remote(whole, whole, n, sibling).wait_send()

    def to_sibling(src, dst, n):
        spread([(0, sibling)], lambda k: src, dst, n, src)

    pieces_of = [slice(j * CHUNK, (j + 1) * CHUNK) for j in range(chunks)]
    halves = [slice(0, SPLIT), slice(SPLIT, width)]

    def load(n, src, dst):
        copy = pltpu.make_async_copy(src, dst, load_sem.at[n])
        copy.start()
        return copy

    load_probe = load(chunks, probe_in, probe)
    load_rows = [
        load(chunks + 1, owner_in, owner),
        load(chunks + 2, slot_in, slot),
    ]
    load_k = [load(j, w_key.at[cols], wk.at[cols]) for j, cols in enumerate(pieces_of)]
    load_rows.append(load(chunks + 3, patches, p))
    load_text = [
        load(chunks + 4, text_in, text),
    ]
    late = chunks + 7
    load_v = [load(late + j, w_value.at[cols], wv.at[cols]) for j, cols in enumerate(pieces_of)]
    load_o = load(late + chunks, w_out, wo)

    barrier = pltpu.get_barrier_semaphore()

    greeted = far_peers + near_peers + rest_peers + y_peers + [(0, sibling)]
    for _, device in greeted:
        pl.semaphore_signal(barrier, inc=1, device_id=device, device_id_type=MESH)

    row_i = lax.broadcasted_iota(jnp.int32, (LANES, width), 0)
    col_i = lax.broadcasted_iota(jnp.int32, (LANES, width), 1)
    first = (row_i & (HEADS - 1)) * head_width
    in_head = (col_i >= first) & (col_i < first + head_width)
    hm[...] = jnp.where(in_head & (row_i < 3 * HEADS), 1.0, 0.0).astype(BF16)
    load_probe.wait()
    q3 = pieces(probe[...].reshape(1, width) / math.sqrt(head_width), 3)
    band = lax.broadcasted_iota(jnp.int32, (3 * HEADS, width), 0) // HEADS
    q_rows = jnp.where(band == 0, q3[0], jnp.where(band == 1, q3[1], q3[2]))
    table = (q_rows * hm[0 : 3 * HEADS, :].astype(F32)).astype(BF16)
    kpr[...] = jnp.zeros_like(kpr)
    for j, cols in enumerate(pieces_of):
        load_k[j].wait()
        kpt = mm_nt(table, wk[cols, :])
        kp = kpt[0:HEADS] + kpt[HEADS : 2 * HEADS] + kpt[2 * HEADS : 3 * HEADS]
        kp_pieces = pieces(kp, 3)
        kp3[:, cols] = jnp.concatenate(kp_pieces, axis=0).astype(BF16)
        kpr[3 * HEADS : 6 * HEADS, cols] = jnp.concatenate(
            [kp_pieces[0], kp_pieces[1], kp_pieces[0]], axis=0
        ).astype(BF16)
    rows16[...] = jnp.zeros_like(rows16)
    tt[...] = jnp.zeros_like(tt)

    load_rows[0].wait()
    load_rows[1].wait()
    own_owner = owner[0, pl.ds(grp, 1), :]
    code = (own_owner & 1) * mine + (own_owner >> 1) * IMG + slot[0, pl.ds(grp, 1), :]
    member = code == lax.broadcasted_iota(jnp.int32, (2 * mine, rows), 0)
    ot_f = jnp.where(member, 1.0, 0.0)
    ot[...] = ot_f.astype(BF16)

    load_rows[2].wait()
    s = mm_nt(kp3[...], p[...])
    scores = s[0:HEADS] + s[HEADS : 2 * HEADS] + s[2 * HEADS : 3 * HEADS]
    st[...] = scores
    lane = lax.broadcasted_iota(jnp.int32, (2 * mine, LANES), 1)
    peak = jnp.zeros((2 * mine, LANES), F32)
    for h in range(HEADS):
        top = jnp.max(jnp.where(member, scores[h : h + 1, :], LOW), axis=1, keepdims=True)
        peak = jnp.where(lane == h, top, peak)
    peak_t = jnp.transpose(peak)[0:HEADS]
    shift = mm(stacked(peak_t, 3), ot[...])
    shift = shift[0:HEADS] + shift[HEADS : 2 * HEADS] + shift[2 * HEADS : 3 * HEADS]
    e_hi, e_lo = pieces(jnp.exp(scores - shift), 2)
    blank = jnp.zeros((HEADS, rows), F32)
    e_pad = jnp.concatenate(
        [blank, e_hi, e_lo, jnp.zeros((LANES - 3 * HEADS, rows), F32)], axis=0
    )
    et[...] = jnp.transpose(e_pad).astype(BF16)
    stats = jnp.where(lane < HEADS, peak, mm(ot[...], et[...]))
    for c in range(2):
        part_own[c, :, width : width + LANES] = stats[c * mine : (c + 1) * mine]
    for copy in load_v:
        copy.wait()
    for cols in halves:
        value = mm(p[...], wv[:, cols])
        v[:, cols] = value
        x_hi, x_lo = pieces(mm(et[...], hm[:, cols]) * value, 2)
        total = mm(ot[...], x_hi.astype(BF16)) + mm(ot[...], x_lo.astype(BF16))
        for c in range(2):
            part_own[c, :, cols] = total[c * mine : (c + 1) * mine]
    for copy in load_text:
        copy.wait()
    t_img[(core * nx + x) * nz + z] = text[...]

    pl.semaphore_wait(barrier, len(greeted))
    part_cols = [slice(width, width + LANES)] + halves
    for j, cols in enumerate(part_cols):
        to_sibling(part_own.at[1 - core, :, cols], part_in.at[:, cols], 16 + j)
    t_here = (core * nx + x) * nz
    slabs = lambda ref, n: ref.at[pl.ds(0, n)]
    spread(z_peers, lambda k: text, t_img.at[t_here + z], 1, slabs(t_img, nz - 1))

    arrived(part_in.at[:, part_cols[0]], 16)
    lane_m = lax.broadcasted_iota(jnp.int32, (mine, LANES), 1)
    stat_a = part_own[core, :, width : width + LANES]
    stat_b = part_in[:, width : width + LANES]
    top = jnp.maximum(stat_a, stat_b)
    chip_stats = jnp.where(lane_m < HEADS, top, 0.0)
    scale = []
    for stat in (stat_a, stat_b):
        f = jnp.where(lane_m < HEADS, jnp.exp(stat - top), 0.0)
        chip_stats += stat * (pltpu.roll(f, HEADS, 1) + pltpu.roll(f, 2 * HEADS, 1))
        f_hi, f_lo = pieces(f, 2)
        scale.append((f_hi + pltpu.roll(f_lo, HEADS, 1)).astype(BF16))
    for k in range(nq):
        acc_out[k, :, width : width + LANES] = chip_stats[k * IMG : (k + 1) * IMG]
    for j, cols in enumerate(halves):
        arrived(part_in.at[:, cols], 17 + j)
        total = (
            mm(scale[0], hm[:, cols]) * part_own[core, :, cols]
            + mm(scale[1], hm[:, cols]) * part_in[:, cols]
        )
        for k in range(nq):
            acc_out[k, :, cols] = total[k * IMG : (k + 1) * IMG]
    spread(far_peers + near_peers, lambda k: acc_out.at[k], acc_in.at[q], 2, slabs(acc_in, nq - 1))
    acc_in[q] = acc_out[q]

    arrived(slabs(t_img, nz - 1), 1)
    x_part = t_img.at[pl.ds(t_here, nz)]
    spread(x_peers, lambda k: x_part, x_part, 3, slabs(t_img, (nx - 1) * nz))
    arrived(slabs(t_img, (nx - 1) * nz), 3)
    t_half = lambda c: t_img.at[pl.ds(c * nx * nz, nx * nz)]
    to_sibling(t_half(core), t_half(core), 4)
    load_o.wait()

    for c in range(2):
        half = ot_f[c * mine : (c + 1) * mine]
        ob[c] = jnp.transpose(jnp.concatenate([half, half], axis=0)).astype(BF16)

    arrived(slabs(acc_in, nq - 1), 2)
    lane4 = lax.broadcasted_iota(jnp.int32, (IMG, LANES), 1)
    heads4 = lane4 < HEADS
    parts = [acc_in[k, :, width : width + LANES] for k in range(nq)]
    m = parts[0]
    for part in parts[1:]:
        m = jnp.maximum(m, part)
    factors = []
    denom = jnp.zeros((IMG, LANES), F32)
    for part in parts:
        f = jnp.exp(part - m)
        mass = pltpu.roll(part, LANES - HEADS, 1) + pltpu.roll(part, LANES - 2 * HEADS, 1)
        factors.append(f)
        denom = denom + f * mass
    denom = jnp.where(heads4, denom, 1.0)
    lse = m + jnp.log(denom)
    for k, f in enumerate(factors):
        f_hi, f_lo = pieces(jnp.where(heads4, f / denom, 0.0), 2)
        fs[k * IMG : (k + 1) * IMG, :] = f_hi + pltpu.roll(f_lo, HEADS, 1)
    factor = mm(fs[...].astype(BF16), hm[...])
    pooled = jnp.zeros((IMG, width), F32)
    for k in range(nq):
        pooled = pooled + factor[k * IMG : (k + 1) * IMG] * acc_in[k, :, 0:width]
    pooled_buf[...] = pooled
    embeds = three(mm(small_rows(pooled, rows16), wo[...]))
    norm = jnp.sqrt(jnp.sum(embeds * embeds, axis=1, keepdims=True) + EPS)
    unit = embeds / norm
    unit_plane[xy] = unit
    u_here = unit_plane.at[xy]
    spread(y_peers, lambda k: u_here, u_here, 5, slabs(unit_plane, ny - 1))

    arrived(t_half(1 - core), 4)
    ntext = 2 * nx * nz * IMG
    for k in range(2 * nx * nz):
        tf[k * IMG : (k + 1) * IMG, :] = t_img[k].astype(F32)
    texts = tf[...]
    tb = texts.astype(BF16)
    inv = 1.0 / jnp.sqrt(jnp.sum(texts * texts, axis=1, keepdims=True) + EPS)
    inv_row = jnp.transpose(jnp.broadcast_to(inv, (ntext, LANES)))[0:1, :]
    temper = jnp.exp(jnp.full((1, 1), logit_scale[0], F32))
    offset = logit_bias[0]

    def block_signal(u_pieces, tb_, inv_, image_slab, text_slab):
        n, t = u_pieces[0].shape[0], tb_.shape[0]
        dots = mm_nt(jnp.concatenate(u_pieces, axis=0).astype(BF16), tb_)
        dots = dots[0:n] + dots[n : 2 * n] + dots[2 * n : 3 * n]
        logits = temper * (dots * inv_) + offset
        row = lax.broadcasted_iota(jnp.int32, (n, t), 0)
        col = lax.broadcasted_iota(jnp.int32, (n, t), 1)
        positive = ((row >> 2) == image_slab) & (col - text_slab * IMG == (row & (IMG - 1)))
        return 1.0 / (1.0 + jnp.exp(-logits)) - jnp.where(positive, 1.0, 0.0)

    arrived(slabs(unit_plane, ny - 1), 5)
    nline = ny * IMG
    for k in range(ny):
        u16[k * IMG : (k + 1) * IMG, :] = unit_plane[k * nx + x]
    signal = block_signal(pieces(u16[...], 3), tb, inv_row, y, (core * nx + x) * nz + z)
    di = mm(stacked(signal * inv_row, 3), tb)
    di = di[0:nline] + di[nline : 2 * nline] + di[2 * nline : 3 * nline]
    for k in range(ny):
        di_out[k] = di[k * IMG : (k + 1) * IMG]
    spread(y_peers, lambda k: di_out.at[k], di_in.at[y], 6, slabs(di_in, ny - 1))
    spread(rest_peers, lambda k: u_here, u_here, 7, slabs(unit_plane, (nx - 1) * ny))
    di_in[y] = di_out[y]

    arrived(slabs(di_in, ny - 1), 6)
    dunit = di_in[0]
    for k in range(1, ny):
        dunit = dunit + di_in[k]
    dunit = dunit * (temper * LOSS_SCALE)
    unit = unit_plane[xy]
    embed_grad = (dunit - unit * jnp.sum(unit * dunit, axis=1, keepdims=True)) / norm
    pooled_grad = three(mm_nt(small_rows(embed_grad, rows16), wo[...]))
    mass = three(mm_nt(small_rows(pooled_grad * pooled_buf[...], rows16), hm[...]))
    pg_all[core, q, :, 0:width] = pooled_grad
    pg_all[core, q, :, width : width + LANES] = jnp.where(
        heads4, lse, jnp.where(lane4 < 2 * HEADS, mass, 0.0)
    )
    early, pending = pending, []
    pg_here = pg_all.at[core, q]
    near = pg_all.at[core, pl.ds(xh * nz, nz)]
    spread(far_peers, lambda k: pg_here, pg_here, 9, pg_all.at[0, pl.ds(0, nq - nz)])
    spread(near_peers, lambda k: pg_here, pg_here, 10, pg_all.at[0, pl.ds(0, nz - 1)])

    arrived(slabs(unit_plane, (nx - 1) * ny), 7)
    for k in range(nxy):
        u64[k * IMG : (k + 1) * IMG, :] = unit_plane[k]
    for c in range(2):
        here = pl.ds(pl.multiple_of((c * nx + x) * nz * IMG, nz * IMG), nz * IMG)
        tt[c * nz * IMG : (c + 1) * nz * IMG, :] = tf[here, :]
    line_texts = tt[...]
    line_inv = 1.0 / jnp.sqrt(jnp.sum(line_texts * line_texts, axis=1, keepdims=True) + EPS)
    line_inv = jnp.transpose(jnp.broadcast_to(line_inv, (LANES, LANES)))[0:1, :]
    u_pieces = pieces(u64[...], 3)
    signal = block_signal(u_pieces, line_texts.astype(BF16), line_inv, xy, core * nz + z)
    s_hi, s_lo = pieces(signal, 2)
    gap = -3 * nxy * IMG % LANES
    s_pad = jnp.concatenate([s_hi, s_hi, s_lo, jnp.zeros((gap, LANES), F32)], axis=0)
    u_pad = jnp.concatenate(
        [u_pieces[0], u_pieces[1], u_pieces[0], jnp.zeros((gap, width), F32)], axis=0
    )
    td = mm(jnp.transpose(s_pad).astype(BF16), u_pad.astype(BF16))
    for c in range(2):
        for k in range(nz):
            r = (c * nz + k) * IMG
            td_out[c, k] = td[r : r + IMG]
    to_sibling(td_out.at[1 - core], td_mid, 8)

    settle(early)

    arrived(pg_all.at[0, pl.ds(0, nz - 1)], 10)
    to_sibling(near, near, 11)
    arrived(td_mid, 8)
    for k in range(nz):
        td_out[core, k] = td_out[core, k] + td_mid[k]
    spread(z_peers, lambda k: td_out.at[core, k], td_in.at[z], 12, slabs(td_in, nz - 1))
    td_in[z] = td_out[core, z]
    arrived(pg_all.at[0, pl.ds(0, nq - nz)], 9)
    for k in range(X_HIGH - 1):
        part = pg_all.at[core, pl.ds(lax.rem(xh + 1 + k, X_HIGH) * nz, nz)]
        to_sibling(part, part, 13 + k)
    for k in range(nq):
        pgm[core, k * IMG : (k + 1) * IMG, :] = pg_all[core, k]
    pgr = mm(ob[core], stacked(pgm[core, :, 0:width], 2))
    arrived(near, 11)
    for k in range(X_HIGH - 1):
        arrived(near, 13 + k)

    def store(j):
        cols = halves[j]
        return pltpu.make_async_copy(out.at[:, cols], g_patch.at[:, cols], load_sem.at[j])

    for k in range(nq):
        pgm[1 - core, k * IMG : (k + 1) * IMG, :] = pg_all[1 - core, k]
    row_stats = jnp.concatenate([pgm[0, :, width:], pgm[1, :, width:]], axis=0)
    row_stats = mm(stacked(jnp.transpose(row_stats)[0 : 2 * HEADS], 3), ot[...])
    row_stats = (
        row_stats[0 : 2 * HEADS] + row_stats[2 * HEADS : 4 * HEADS] + row_stats[4 * HEADS : 6 * HEADS]
    )
    pgr = pgr + mm(ob[1 - core], stacked(pgm[1 - core, :, 0:width], 2))
    w = jnp.exp(st[...] - row_stats[0:HEADS])
    gap = jnp.zeros((LANES - 2 * HEADS, rows), F32)
    w_t = jnp.transpose(jnp.concatenate(pieces(w, 2) + [gap], axis=0)).astype(BF16)
    vg[...] = stacked(mm(w_t, hm[...]) * pgr, 2)
    d_hi, d_lo = pieces(pgr * v[...], 2)
    dw = mm_nt(hm[0:HEADS, :], d_hi.astype(BF16)) + mm_nt(hm[0:HEADS, :], d_lo.astype(BF16))
    ds_hi, ds_lo = pieces(w * (dw - row_stats[HEADS : 2 * HEADS]), 2)
    ds_t = jnp.transpose(
        jnp.concatenate([blank, blank, blank, ds_hi, ds_hi, ds_lo, blank, blank], axis=0)
    ).astype(BF16)

    for j, cols in enumerate(halves):
        g = mm_nt(vg[...], wv[cols, :])
        g = g[0:rows] + g[rows : 2 * rows] + mm(ds_t, kpr[:, cols])
        out[:, cols] = g.astype(BF16)
        store(j).start()

    arrived(slabs(td_in, nz - 1), 12)
    text_dunit = td_in[0]
    for k in range(1, nz):
        text_dunit = text_dunit + td_in[k]
    text_dunit = text_dunit * (temper * LOSS_SCALE)
    own_text = text[...].astype(F32)
    text_norm = jnp.sqrt(jnp.sum(own_text * own_text, axis=1, keepdims=True) + EPS)
    text_unit = own_text / text_norm
    text_out[...] = (
        (text_dunit - text_unit * jnp.sum(text_unit * text_dunit, axis=1, keepdims=True))
        / text_norm
    ).astype(BF16)

    store_text = pltpu.make_async_copy(text_out, g_text, load_sem.at[len(halves)])
    store_text.start()
    settle(pending)
    for j in range(len(halves)):
        store(j).wait()
    store_text.wait()


def hand_over(patch_in, text_in, patch_out, text_out, patch, text, sem):
    rows = patch.shape[0] // 2
    halves = [slice(0, rows), slice(rows, 2 * rows)]
    here = [
        (patch_in.at[halves[0]], patch.at[halves[0]], patch_out.at[halves[0]]),
        (patch_in.at[halves[1]], patch.at[halves[1]], patch_out.at[halves[1]]),
        (text_in, text, text_out),
    ]
    first = [pltpu.make_async_copy(a, b, sem.at[k]) for k, (a, b, _) in enumerate(here)]
    then = [pltpu.make_async_copy(b, c, sem.at[3 + k]) for k, (_, b, c) in enumerate(here)]
    for copy in first:
        copy.start()
    for arrived, copy in zip(first, then):
        arrived.wait()
        copy.start()
    for copy in then:
        copy.wait()


def local(nb, ng, patches, owner, slot, text, probe, w_key, w_value, w_out, scale, bias):
    rows, width = patches.shape
    nq = ng // 2
    nz = nq // X_HIGH
    nx = X_LOW * X_HIGH
    ny = nb // X_LOW
    nxy = nx * ny
    mine = nq * IMG
    wide = width + LANES
    anywhere = pl.BlockSpec(memory_space=pl.ANY)
    weight = pltpu.VMEM((width, width), BF16)
    dma = pltpu.SemaphoreType.DMA
    shapes = (
        jax.ShapeDtypeStruct((rows, width), BF16),
        jax.ShapeDtypeStruct((IMG, width), BF16),
    )
    grads = pl.pallas_call(
        functools.partial(kernel, nb, ng),
        out_shape=shapes,
        in_specs=[anywhere] * 8 + [pl.BlockSpec(memory_space=pltpu.SMEM)] * 2,
        out_specs=(anywhere, anywhere),
        scratch_shapes=[
            pltpu.VMEM(owner.shape, jnp.int32),
            pltpu.VMEM(slot.shape, jnp.int32),
            pltpu.VMEM(text.shape, BF16),
            pltpu.VMEM((width,), F32),
            weight,
            weight,
            weight,
            pltpu.VMEM((rows, width), BF16),
            pltpu.VMEM((rows, width), F32),
            pltpu.VMEM((HEADS, rows), F32),
            pltpu.VMEM((LANES, width), BF16),
            pltpu.VMEM((3 * HEADS, width), BF16),
            pltpu.VMEM((LANES, width), BF16),
            pltpu.VMEM((2 * mine, rows), BF16),
            pltpu.VMEM((rows, LANES), BF16),
            pltpu.VMEM((2, rows, 2 * mine), BF16),
            pltpu.VMEM((2, mine, wide), F32),
            pltpu.VMEM((mine, wide), F32),
            pltpu.VMEM((nq, IMG, wide), F32),
            pltpu.VMEM((nq, IMG, wide), F32),
            pltpu.VMEM((mine, LANES), F32),
            pltpu.VMEM((16, width), F32),
            pltpu.VMEM((IMG, width), F32),
            pltpu.VMEM((nxy, IMG, width), F32),
            pltpu.VMEM((ny * IMG, width), F32),
            pltpu.VMEM((ny, IMG, width), F32),
            pltpu.VMEM((ny, IMG, width), F32),
            pltpu.VMEM((nxy * IMG, width), F32),
            pltpu.VMEM((2 * nx * nz, IMG, width), BF16),
            pltpu.VMEM((2 * nx * nz * IMG, width), F32),
            pltpu.VMEM((LANES, width), F32),
            pltpu.VMEM((2, nz, IMG, width), F32),
            pltpu.VMEM((nz, IMG, width), F32),
            pltpu.VMEM((nz, IMG, width), F32),
            pltpu.VMEM((2, nq, IMG, wide), F32),
            pltpu.VMEM((2, mine, wide), F32),
            pltpu.VMEM((2 * rows, width), BF16),
            pltpu.VMEM((rows, width), BF16),
            pltpu.VMEM(text.shape, BF16),
            dma((16,)),
            dma((20,)),
            dma((20,)),
        ],
        compiler_params=pltpu.CompilerParams(
            collective_id=0, has_side_effects=True, vmem_limit_bytes=56 * 2**20
        ),
        name="pool_contrast",
    )(patches, owner, slot, text, probe, w_key, w_value, w_out, scale, bias)
    return pl.pallas_call(
        hand_over,
        out_shape=shapes,
        in_specs=[anywhere, anywhere],
        out_specs=(anywhere, anywhere),
        scratch_shapes=[
            pltpu.VMEM((rows, width), BF16),
            pltpu.VMEM(text.shape, BF16),
            dma((6,)),
        ],
        compiler_params=pltpu.CompilerParams(vmem_limit_bytes=56 * 2**20),
        name="hand_over",
    )(*grads)


def solution(mesh):
    nb = mesh.shape["blk"]
    ng = mesh.shape["group"]
    return jax.shard_map(
        functools.partial(local, nb, ng),
        mesh=mesh,
        in_specs=(
            P(("blk", "group"), None),
            P("blk", None, None),
            P("blk", None, None),
            P(("blk", "group"), None),
            P(),
            P(),
            P(),
            P(),
            P(),
            P(),
        ),
        out_specs=(P(("blk", "group"), None), P(("blk", "group"), None)),
        check_vma=False,
    )
```

```python
import functools
import math

import jax
import jax.numpy as jnp
from jax import lax
from jax.experimental import pallas as pl
from jax.experimental.pallas import tpu as pltpu
from jax.sharding import PartitionSpec as P

HEADS = 16
IMG = 4
X_LOW, X_HIGH = 2, 2
LANES = 128
CHUNK = 384
SPLIT = 640
LOSS_SCALE = 256.0
EPS = 1e-06
LOW = -1e30

F32 = jnp.float32
BF16 = jnp.bfloat16
MESH = pl.DeviceIdType.MESH


def mm(a, b):
    return lax.dot_general(a, b, (((1,), (0,)), ((), ())), preferred_element_type=F32)


def mm_nt(a, b):
    return lax.dot_general(a, b, (((1,), (1,)), ((), ())), preferred_element_type=F32)


def pieces(x, count):
    out = []
    for _ in range(count - 1):
        top = x.astype(BF16).astype(F32)
        out.append(top)
        x = x - top
    out.append(x.astype(BF16).astype(F32))
    return out


def stacked(x, count):
    return jnp.concatenate(pieces(x, count), axis=0).astype(BF16)


def small_rows(x, buf):
    for k, piece in enumerate(pieces(x, 3)):
        buf[k * IMG : (k + 1) * IMG, :] = piece
    return buf[...].astype(BF16)


def three(y):
    return y[0:IMG] + y[IMG : 2 * IMG] + y[2 * IMG : 3 * IMG]


def far(n):
    return [(n // 2 + ((j + 1) // 2) * (2 * ((j + 1) % 2) - 1)) % n for j in range(n)]


def kernel(
    nb,
    ng,
    patches,
    owner_in,
    slot_in,
    text_in,
    probe_in,
    w_key,
    w_value,
    w_out,
    logit_scale,
    logit_bias,
    g_patch,
    g_text,
    owner,
    slot,
    text,
    probe,
    wk,
    wv,
    wo,
    p,
    v,
    st,
    hm,
    kp3,
    kpr,
    ot,
    et,
    ob,
    part_own,
    part_in,
    acc_out,
    acc_in,
    fs,
    rows16,
    pooled_buf,
    unit_plane,
    u16,
    di_out,
    di_in,
    u64,
    t_img,
    tf,
    tt,
    td_out,
    td_mid,
    td_in,
    pg_all,
    pgm,
    vg,
    out,
    text_out,
    load_sem,
    send_sem,
    recv_sem,
):
    nq = ng // 2
    nz = nq // X_HIGH
    nx = X_LOW * X_HIGH
    ny = nb // X_LOW
    nxy = nx * ny
    mine = nq * IMG
    rows, width = patches.shape
    chunks = width // CHUNK
    head_width = width // HEADS
    blk = lax.axis_index("blk")
    grp = lax.axis_index("group")
    core = lax.rem(grp, 2)
    q = lax.div(grp, 2)
    z = lax.rem(q, nz)
    xh = lax.div(q, nz)
    y = lax.div(blk, X_LOW)
    x = xh * X_LOW + lax.rem(blk, X_LOW)
    xy = y * nx + x
    pending = []

    def at(x_, y_, z_, c_):
        x_high = lax.div(x_, X_LOW)
        return (y_ * X_LOW + x_ - x_high * X_LOW, (x_high * nz + z_) * 2 + c_)

    def ring(pos, n):
        return [pos if d == 0 else lax.rem(pos + d, n) for d in far(n)]

    sibling = at(x, y, z, 1 - core)
    ring_x, ring_y, ring_z = ring(x, nx), ring(y, ny), ring(z, nz)
    z_peers = [(k, at(x, y, k, core)) for k in ring_z[:-1]]
    x_peers = [(k, at(k, y, z, core)) for k in ring_x[:-1]]
    y_peers = [(k, at(x, k, z, core)) for k in ring_y[:-1]]
    rest_peers = [(j * nx + k, at(k, j, z, core)) for k in ring_x[:-1] for j in ring_y]
    far_peers = [
        (h * nz + k, (blk, (h * nz + k) * 2 + core)) for h in ring(xh, X_HIGH)[:-1] for k in ring_z
    ]
    near_peers = [(xh * nz + k, device) for k, device in z_peers]

    def remote(src, dst, n, device):
        return pltpu.make_async_remote_copy(
            src_ref=src,
            dst_ref=dst,
            send_sem=send_sem.at[n],
            recv_sem=recv_sem.at[n],
            device_id=device,
            device_id_type=MESH,
        )

    def spread(peers, src_of, dst, n, whole):
        for k, device in peers:
            remote(src_of(k), dst, n, device).start()
        pending.append((whole, n))

    def arrived(whole, n):
        remote(whole, whole, n, sibling).wait_recv()

    def settle(sends):
        for whole, n in sends:
            remote(whole, whole, n, sibling).wait_send()

    def to_sibling(src, dst, n):
        spread([(0, sibling)], lambda k: src, dst, n, src)

    pieces_of = [slice(j * CHUNK, (j + 1) * CHUNK) for j in range(chunks)]
    halves = [slice(0, SPLIT), slice(SPLIT, width)]

    def load(n, src, dst):
        copy = pltpu.make_async_copy(src, dst, load_sem.at[n])
        copy.start()
        return copy

    load_probe = load(chunks, probe_in, probe)
    load_rows = [
        load(chunks + 1, owner_in, owner),
        load(chunks + 2, slot_in, slot),
    ]
    load_k = [load(j, w_key.at[cols], wk.at[cols]) for j, cols in enumerate(pieces_of)]
    load_rows.append(load(chunks + 3, patches, p))
    load_text = [
        load(chunks + 4, text_in, text),
    ]
    late = chunks + 7
    load_v = [load(late + j, w_value.at[cols], wv.at[cols]) for j, cols in enumerate(pieces_of)]
    load_o = load(late + chunks, w_out, wo)

    barrier = pltpu.get_barrier_semaphore()

    greeted = far_peers + near_peers + rest_peers + y_peers + [(0, sibling)]
    for _, device in greeted:
        pl.semaphore_signal(barrier, inc=1, device_id=device, device_id_type=MESH)

    row_i = lax.broadcasted_iota(jnp.int32, (LANES, width), 0)
    col_i = lax.broadcasted_iota(jnp.int32, (LANES, width), 1)
    first = (row_i & (HEADS - 1)) * head_width
    in_head = (col_i >= first) & (col_i < first + head_width)
    hm[...] = jnp.where(in_head & (row_i < 3 * HEADS), 1.0, 0.0).astype(BF16)
    load_probe.wait()
    q3 = pieces(probe[...].reshape(1, width) / math.sqrt(head_width), 3)
    band = lax.broadcasted_iota(jnp.int32, (3 * HEADS, width), 0) // HEADS
    q_rows = jnp.where(band == 0, q3[0], jnp.where(band == 1, q3[1], q3[2]))
    table = (q_rows * hm[0 : 3 * HEADS, :].astype(F32)).astype(BF16)
    kpr[...] = jnp.zeros_like(kpr)
    for j, cols in enumerate(pieces_of):
        load_k[j].wait()
        kpt = mm_nt(table, wk[cols, :])
        kp = kpt[0:HEADS] + kpt[HEADS : 2 * HEADS] + kpt[2 * HEADS : 3 * HEADS]
        kp_pieces = pieces(kp, 3)
        kp3[:, cols] = jnp.concatenate(kp_pieces, axis=0).astype(BF16)
        kpr[3 * HEADS : 6 * HEADS, cols] = jnp.concatenate(
            [kp_pieces[0], kp_pieces[1], kp_pieces[0]], axis=0
        ).astype(BF16)
    rows16[...] = jnp.zeros_like(rows16)
    tt[...] = jnp.zeros_like(tt)

    load_rows[0].wait()
    load_rows[1].wait()
    own_owner = owner[0, pl.ds(grp, 1), :]
    code = (own_owner & 1) * mine + (own_owner >> 1) * IMG + slot[0, pl.ds(grp, 1), :]
    member = code == lax.broadcasted_iota(jnp.int32, (2 * mine, rows), 0)
    ot_f = jnp.where(member, 1.0, 0.0)
    ot[...] = ot_f.astype(BF16)

    load_rows[2].wait()
    s = mm_nt(kp3[...], p[...])
    scores = s[0:HEADS] + s[HEADS : 2 * HEADS] + s[2 * HEADS : 3 * HEADS]
    st[...] = scores
    lane = lax.broadcasted_iota(jnp.int32, (2 * mine, LANES), 1)
    peak = jnp.zeros((2 * mine, LANES), F32)
    for h in range(HEADS):
        top = jnp.max(jnp.where(member, scores[h : h + 1, :], LOW), axis=1, keepdims=True)
        peak = jnp.where(lane == h, top, peak)
    peak_t = jnp.transpose(peak)[0:HEADS]
    shift = mm(stacked(peak_t, 3), ot[...])
    shift = shift[0:HEADS] + shift[HEADS : 2 * HEADS] + shift[2 * HEADS : 3 * HEADS]
    e_hi, e_lo = pieces(jnp.exp(scores - shift), 2)
    blank = jnp.zeros((HEADS, rows), F32)
    e_pad = jnp.concatenate(
        [blank, e_hi, e_lo, jnp.zeros((LANES - 3 * HEADS, rows), F32)], axis=0
    )
    et[...] = jnp.transpose(e_pad).astype(BF16)
    stats = jnp.where(lane < HEADS, peak, mm(ot[...], et[...]))
    for c in range(2):
        part_own[c, :, width : width + LANES] = stats[c * mine : (c + 1) * mine]
    for copy in load_v:
        copy.wait()
    for cols in halves:
        value = mm(p[...], wv[:, cols])
        v[:, cols] = value
        x_hi, x_lo = pieces(mm(et[...], hm[:, cols]) * value, 2)
        total = mm(ot[...], x_hi.astype(BF16)) + mm(ot[...], x_lo.astype(BF16))
        for c in range(2):
            part_own[c, :, cols] = total[c * mine : (c + 1) * mine]
    for copy in load_text:
        copy.wait()
    t_img[(core * nx + x) * nz + z] = text[...]

    pl.semaphore_wait(barrier, len(greeted))
    part_cols = [slice(width, width + LANES)] + halves
    for j, cols in enumerate(part_cols):
        to_sibling(part_own.at[1 - core, :, cols], part_in.at[:, cols], 16 + j)
    t_here = (core * nx + x) * nz
    slabs = lambda ref, n: ref.at[pl.ds(0, n)]
    spread(z_peers, lambda k: text, t_img.at[t_here + z], 1, slabs(t_img, nz - 1))

    arrived(part_in.at[:, part_cols[0]], 16)
    lane_m = lax.broadcasted_iota(jnp.int32, (mine, LANES), 1)
    stat_a = part_own[core, :, width : width + LANES]
    stat_b = part_in[:, width : width + LANES]
    top = jnp.maximum(stat_a, stat_b)
    chip_stats = jnp.where(lane_m < HEADS, top, 0.0)
    scale = []
    for stat in (stat_a, stat_b):
        f = jnp.where(lane_m < HEADS, jnp.exp(stat - top), 0.0)
        chip_stats += stat * (pltpu.roll(f, HEADS, 1) + pltpu.roll(f, 2 * HEADS, 1))
        f_hi, f_lo = pieces(f, 2)
        scale.append((f_hi + pltpu.roll(f_lo, HEADS, 1)).astype(BF16))
    for k in range(nq):
        acc_out[k, :, width : width + LANES] = chip_stats[k * IMG : (k + 1) * IMG]
    for j, cols in enumerate(halves):
        arrived(part_in.at[:, cols], 17 + j)
        total = (
            mm(scale[0], hm[:, cols]) * part_own[core, :, cols]
            + mm(scale[1], hm[:, cols]) * part_in[:, cols]
        )
        for k in range(nq):
            acc_out[k, :, cols] = total[k * IMG : (k + 1) * IMG]
    spread(far_peers + near_peers, lambda k: acc_out.at[k], acc_in.at[q], 2, slabs(acc_in, nq - 1))
    acc_in[q] = acc_out[q]

    arrived(slabs(t_img, nz - 1), 1)
    x_part = t_img.at[pl.ds(t_here, nz)]
    spread(x_peers, lambda k: x_part, x_part, 3, slabs(t_img, (nx - 1) * nz))
    arrived(slabs(t_img, (nx - 1) * nz), 3)
    t_half = lambda c: t_img.at[pl.ds(c * nx * nz, nx * nz)]
    to_sibling(t_half(core), t_half(core), 4)
    load_o.wait()

    for c in range(2):
        half = ot_f[c * mine : (c + 1) * mine]
        ob[c] = jnp.transpose(jnp.concatenate([half, half], axis=0)).astype(BF16)

    arrived(slabs(acc_in, nq - 1), 2)
    lane4 = lax.broadcasted_iota(jnp.int32, (IMG, LANES), 1)
    heads4 = lane4 < HEADS
    parts = [acc_in[k, :, width : width + LANES] for k in range(nq)]
    m = parts[0]
    for part in parts[1:]:
        m = jnp.maximum(m, part)
    factors = []
    denom = jnp.zeros((IMG, LANES), F32)
    for part in parts:
        f = jnp.exp(part - m)
        mass = pltpu.roll(part, LANES - HEADS, 1) + pltpu.roll(part, LANES - 2 * HEADS, 1)
        factors.append(f)
        denom = denom + f * mass
    denom = jnp.where(heads4, denom, 1.0)
    lse = m + jnp.log(denom)
    for k, f in enumerate(factors):
        f_hi, f_lo = pieces(jnp.where(heads4, f / denom, 0.0), 2)
        fs[k * IMG : (k + 1) * IMG, :] = f_hi + pltpu.roll(f_lo, HEADS, 1)
    factor = mm(fs[...].astype(BF16), hm[...])
    pooled = jnp.zeros((IMG, width), F32)
    for k in range(nq):
        pooled = pooled + factor[k * IMG : (k + 1) * IMG] * acc_in[k, :, 0:width]
    pooled_buf[...] = pooled
    embeds = three(mm(small_rows(pooled, rows16), wo[...]))
    norm = jnp.sqrt(jnp.sum(embeds * embeds, axis=1, keepdims=True) + EPS)
    unit = embeds / norm
    unit_plane[xy] = unit
    u_here = unit_plane.at[xy]
    spread(y_peers, lambda k: u_here, u_here, 5, slabs(unit_plane, ny - 1))

    arrived(t_half(1 - core), 4)
    ntext = 2 * nx * nz * IMG
    for k in range(2 * nx * nz):
        tf[k * IMG : (k + 1) * IMG, :] = t_img[k].astype(F32)
    texts = tf[...]
    tb = texts.astype(BF16)
    inv = 1.0 / jnp.sqrt(jnp.sum(texts * texts, axis=1, keepdims=True) + EPS)
    inv_row = jnp.transpose(jnp.broadcast_to(inv, (ntext, LANES)))[0:1, :]
    temper = jnp.exp(jnp.full((1, 1), logit_scale[0], F32))
    offset = logit_bias[0]

    def block_signal(u_pieces, tb_, inv_, image_slab, text_slab):
        n, t = u_pieces[0].shape[0], tb_.shape[0]
        dots = mm_nt(jnp.concatenate(u_pieces, axis=0).astype(BF16), tb_)
        dots = dots[0:n] + dots[n : 2 * n] + dots[2 * n : 3 * n]
        logits = temper * (dots * inv_) + offset
        row = lax.broadcasted_iota(jnp.int32, (n, t), 0)
        col = lax.broadcasted_iota(jnp.int32, (n, t), 1)
        positive = ((row >> 2) == image_slab) & (col - text_slab * IMG == (row & (IMG - 1)))
        return 1.0 / (1.0 + jnp.exp(-logits)) - jnp.where(positive, 1.0, 0.0)

    arrived(slabs(unit_plane, ny - 1), 5)
    nline = ny * IMG
    for k in range(ny):
        u16[k * IMG : (k + 1) * IMG, :] = unit_plane[k * nx + x]
    signal = block_signal(pieces(u16[...], 3), tb, inv_row, y, (core * nx + x) * nz + z)
    di = mm(stacked(signal * inv_row, 3), tb)
    di = di[0:nline] + di[nline : 2 * nline] + di[2 * nline : 3 * nline]
    for k in range(ny):
        di_out[k] = di[k * IMG : (k + 1) * IMG]
    spread(y_peers, lambda k: di_out.at[k], di_in.at[y], 6, slabs(di_in, ny - 1))
    spread(rest_peers, lambda k: u_here, u_here, 7, slabs(unit_plane, (nx - 1) * ny))
    di_in[y] = di_out[y]

    arrived(slabs(di_in, ny - 1), 6)
    dunit = di_in[0]
    for k in range(1, ny):
        dunit = dunit + di_in[k]
    dunit = dunit * (temper * LOSS_SCALE)
    unit = unit_plane[xy]
    embed_grad = (dunit - unit * jnp.sum(unit * dunit, axis=1, keepdims=True)) / norm
    pooled_grad = three(mm_nt(small_rows(embed_grad, rows16), wo[...]))
    mass = three(mm_nt(small_rows(pooled_grad * pooled_buf[...], rows16), hm[...]))
    pg_all[core, q, :, 0:width] = pooled_grad
    pg_all[core, q, :, width : width + LANES] = jnp.where(
        heads4, lse, jnp.where(lane4 < 2 * HEADS, mass, 0.0)
    )
    early, pending = pending, []
    pg_here = pg_all.at[core, q]
    near = pg_all.at[core, pl.ds(xh * nz, nz)]
    spread(far_peers, lambda k: pg_here, pg_here, 9, pg_all.at[0, pl.ds(0, nq - nz)])
    spread(near_peers, lambda k: pg_here, pg_here, 10, pg_all.at[0, pl.ds(0, nz - 1)])

    arrived(slabs(unit_plane, (nx - 1) * ny), 7)
    for k in range(nxy):
        u64[k * IMG : (k + 1) * IMG, :] = unit_plane[k]
    for c in range(2):
        here = pl.ds(pl.multiple_of((c * nx + x) * nz * IMG, nz * IMG), nz * IMG)
        tt[c * nz * IMG : (c + 1) * nz * IMG, :] = tf[here, :]
    line_texts = tt[...]
    line_inv = 1.0 / jnp.sqrt(jnp.sum(line_texts * line_texts, axis=1, keepdims=True) + EPS)
    line_inv = jnp.transpose(jnp.broadcast_to(line_inv, (LANES, LANES)))[0:1, :]
    u_pieces = pieces(u64[...], 3)
    signal = block_signal(u_pieces, line_texts.astype(BF16), line_inv, xy, core * nz + z)
    s_hi, s_lo = pieces(signal, 2)
    gap = -3 * nxy * IMG % LANES
    s_pad = jnp.concatenate([s_hi, s_hi, s_lo, jnp.zeros((gap, LANES), F32)], axis=0)
    u_pad = jnp.concatenate(
        [u_pieces[0], u_pieces[1], u_pieces[0], jnp.zeros((gap, width), F32)], axis=0
    )
    td = mm(jnp.transpose(s_pad).astype(BF16), u_pad.astype(BF16))
    for c in range(2):
        for k in range(nz):
            r = (c * nz + k) * IMG
            td_out[c, k] = td[r : r + IMG]
    to_sibling(td_out.at[1 - core], td_mid, 8)

    settle(early)

    arrived(pg_all.at[0, pl.ds(0, nz - 1)], 10)
    to_sibling(near, near, 11)
    arrived(td_mid, 8)
    for k in range(nz):
        td_out[core, k] = td_out[core, k] + td_mid[k]
    spread(z_peers, lambda k: td_out.at[core, k], td_in.at[z], 12, slabs(td_in, nz - 1))
    td_in[z] = td_out[core, z]
    arrived(pg_all.at[0, pl.ds(0, nq - nz)], 9)
    for k in range(X_HIGH - 1):
        part = pg_all.at[core, pl.ds(lax.rem(xh + 1 + k, X_HIGH) * nz, nz)]
        to_sibling(part, part, 13 + k)
    for k in range(nq):
        pgm[core, k * IMG : (k + 1) * IMG, :] = pg_all[core, k]
    pgr = mm(ob[core], stacked(pgm[core, :, 0:width], 2))
    arrived(near, 11)
    for k in range(X_HIGH - 1):
        arrived(near, 13 + k)

    def store(j):
        cols = halves[j]
        return pltpu.make_async_copy(out.at[:, cols], g_patch.at[:, cols], load_sem.at[j])

    for k in range(nq):
        pgm[1 - core, k * IMG : (k + 1) * IMG, :] = pg_all[1 - core, k]
    row_stats = jnp.concatenate([pgm[0, :, width:], pgm[1, :, width:]], axis=0)
    row_stats = mm(stacked(jnp.transpose(row_stats)[0 : 2 * HEADS], 3), ot[...])
    row_stats = (
        row_stats[0 : 2 * HEADS] + row_stats[2 * HEADS : 4 * HEADS] + row_stats[4 * HEADS : 6 * HEADS]
    )
    pgr = pgr + mm(ob[1 - core], stacked(pgm[1 - core, :, 0:width], 2))
    w = jnp.exp(st[...] - row_stats[0:HEADS])
    gap = jnp.zeros((LANES - 2 * HEADS, rows), F32)
    w_t = jnp.transpose(jnp.concatenate(pieces(w, 2) + [gap], axis=0)).astype(BF16)
    vg[...] = stacked(mm(w_t, hm[...]) * pgr, 2)
    d_hi, d_lo = pieces(pgr * v[...], 2)
    dw = mm_nt(hm[0:HEADS, :], d_hi.astype(BF16)) + mm_nt(hm[0:HEADS, :], d_lo.astype(BF16))
    ds_hi, ds_lo = pieces(w * (dw - row_stats[HEADS : 2 * HEADS]), 2)
    ds_t = jnp.transpose(
        jnp.concatenate([blank, blank, blank, ds_hi, ds_hi, ds_lo, blank, blank], axis=0)
    ).astype(BF16)

    for j, cols in enumerate(halves):
        g = mm_nt(vg[...], wv[cols, :])
        g = g[0:rows] + g[rows : 2 * rows] + mm(ds_t, kpr[:, cols])
        out[:, cols] = g.astype(BF16)
        store(j).start()

    arrived(slabs(td_in, nz - 1), 12)
    text_dunit = td_in[0]
    for k in range(1, nz):
        text_dunit = text_dunit + td_in[k]
    text_dunit = text_dunit * (temper * LOSS_SCALE)
    own_text = text[...].astype(F32)
    text_norm = jnp.sqrt(jnp.sum(own_text * own_text, axis=1, keepdims=True) + EPS)
    text_unit = own_text / text_norm
    text_out[...] = (
        (text_dunit - text_unit * jnp.sum(text_unit * text_dunit, axis=1, keepdims=True))
        / text_norm
    ).astype(BF16)

    store_text = pltpu.make_async_copy(text_out, g_text, load_sem.at[len(halves)])
    store_text.start()
    settle(pending)
    for j in range(len(halves)):
        store(j).wait()
    store_text.wait()


def hand_over(patch_in, text_in, patch_out, text_out, patch, text, sem):
    rows = patch.shape[0] // 4
    parts = [slice(k * rows, (k + 1) * rows) for k in range(4)]
    here = [(patch_in.at[part], patch.at[part], patch_out.at[part]) for part in parts]
    here.append((text_in, text, text_out))
    first = [pltpu.make_async_copy(a, b, sem.at[k]) for k, (a, b, _) in enumerate(here)]
    then = [pltpu.make_async_copy(b, c, sem.at[5 + k]) for k, (_, b, c) in enumerate(here)]
    for copy in first:
        copy.start()
    for arrived, copy in zip(first, then):
        arrived.wait()
        copy.start()
    for copy in then:
        copy.wait()


def local(nb, ng, patches, owner, slot, text, probe, w_key, w_value, w_out, scale, bias):
    rows, width = patches.shape
    nq = ng // 2
    nz = nq // X_HIGH
    nx = X_LOW * X_HIGH
    ny = nb // X_LOW
    nxy = nx * ny
    mine = nq * IMG
    wide = width + LANES
    anywhere = pl.BlockSpec(memory_space=pl.ANY)
    weight = pltpu.VMEM((width, width), BF16)
    dma = pltpu.SemaphoreType.DMA
    shapes = (
        jax.ShapeDtypeStruct((rows, width), BF16),
        jax.ShapeDtypeStruct((IMG, width), BF16),
    )
    grads = pl.pallas_call(
        functools.partial(kernel, nb, ng),
        out_shape=shapes,
        in_specs=[anywhere] * 8 + [pl.BlockSpec(memory_space=pltpu.SMEM)] * 2,
        out_specs=(anywhere, anywhere),
        scratch_shapes=[
            pltpu.VMEM(owner.shape, jnp.int32),
            pltpu.VMEM(slot.shape, jnp.int32),
            pltpu.VMEM(text.shape, BF16),
            pltpu.VMEM((width,), F32),
            weight,
            weight,
            weight,
            pltpu.VMEM((rows, width), BF16),
            pltpu.VMEM((rows, width), F32),
            pltpu.VMEM((HEADS, rows), F32),
            pltpu.VMEM((LANES, width), BF16),
            pltpu.VMEM((3 * HEADS, width), BF16),
            pltpu.VMEM((LANES, width), BF16),
            pltpu.VMEM((2 * mine, rows), BF16),
            pltpu.VMEM((rows, LANES), BF16),
            pltpu.VMEM((2, rows, 2 * mine), BF16),
            pltpu.VMEM((2, mine, wide), F32),
            pltpu.VMEM((mine, wide), F32),
            pltpu.VMEM((nq, IMG, wide), F32),
            pltpu.VMEM((nq, IMG, wide), F32),
            pltpu.VMEM((mine, LANES), F32),
            pltpu.VMEM((16, width), F32),
            pltpu.VMEM((IMG, width), F32),
            pltpu.VMEM((nxy, IMG, width), F32),
            pltpu.VMEM((ny * IMG, width), F32),
            pltpu.VMEM((ny, IMG, width), F32),
            pltpu.VMEM((ny, IMG, width), F32),
            pltpu.VMEM((nxy * IMG, width), F32),
            pltpu.VMEM((2 * nx * nz, IMG, width), BF16),
            pltpu.VMEM((2 * nx * nz * IMG, width), F32),
            pltpu.VMEM((LANES, width), F32),
            pltpu.VMEM((2, nz, IMG, width), F32),
            pltpu.VMEM((nz, IMG, width), F32),
            pltpu.VMEM((nz, IMG, width), F32),
            pltpu.VMEM((2, nq, IMG, wide), F32),
            pltpu.VMEM((2, mine, wide), F32),
            pltpu.VMEM((2 * rows, width), BF16),
            pltpu.VMEM((rows, width), BF16),
            pltpu.VMEM(text.shape, BF16),
            dma((16,)),
            dma((20,)),
            dma((20,)),
        ],
        compiler_params=pltpu.CompilerParams(
            collective_id=0, has_side_effects=True, vmem_limit_bytes=56 * 2**20
        ),
        name="pool_contrast",
    )(patches, owner, slot, text, probe, w_key, w_value, w_out, scale, bias)
    return pl.pallas_call(
        hand_over,
        out_shape=shapes,
        in_specs=[anywhere, anywhere],
        out_specs=(anywhere, anywhere),
        scratch_shapes=[
            pltpu.VMEM((rows, width), BF16),
            pltpu.VMEM(text.shape, BF16),
            dma((10,)),
        ],
        compiler_params=pltpu.CompilerParams(vmem_limit_bytes=56 * 2**20),
        name="hand_over",
    )(*grads)


def solution(mesh):
    nb = mesh.shape["blk"]
    ng = mesh.shape["group"]
    return jax.shard_map(
        functools.partial(local, nb, ng),
        mesh=mesh,
        in_specs=(
            P(("blk", "group"), None),
            P("blk", None, None),
            P("blk", None, None),
            P(("blk", "group"), None),
            P(),
            P(),
            P(),
            P(),
            P(),
            P(),
        ),
        out_specs=(P(("blk", "group"), None), P(("blk", "group"), None)),
        check_vma=False,
    )
```
